768 devices in a mesh: graph: 32 (over y, z_hi), feat: 24 (over x, z_lo, core).
Axes of the slice: x: 4, y: 8, z: 12 (z_hi: 4, z_lo: 3; z = z_hi * 3 + z_lo), core: 2. Of those that a mesh axis runs over, the one named last changes fastest.
Arguments:
- features: bfloat16 [98304, 576], P('graph', 'feat'), may hold values from -6 to 6
- adjacency: bfloat16 [98304, 384], P('graph'), may hold values from 0 to 3, as said below
- w_self: bfloat16 [576, 512], replicated, may hold values from -0.25 to 0.25
- w_neigh: bfloat16 [576, 512], replicated, may hold values from -0.5 to 0.5
- bias_out: float32 [512], replicated, may hold values from -3 to 3
- cotangent: bfloat16 [98304, 512], P(('graph', 'feat')), may hold values from -6 to 6
Outputs:
- activation: bfloat16 [98304, 512], P(('graph', 'feat'))
- grad_self: float32 [576, 512], replicated
- grad_neigh: float32 [576, 512], replicated
- grad_bias: float32 [512], replicated
- grad_feat: float32 [98304, 576], P('graph', 'feat')
The draws below stay inside these ranges and needn't reach their ends.
Inputs may be any that keep to these rules, and one draw needn't show every extreme that they name: adjacency holds whole numbers and is the band of a symmetric matrix with a zero diagonal: adjacency[i, c] equals the entry of node (i // 128 - 1) * 128 + c for node i, and it is zero where that node lies outside 0 to 98303.
All inputs are finite; a program needn't handle non-finite values.
Results may differ from the reference program's by a relative error of at most 0.007.
Values may be sent and summed in bfloat16 or wider, within the bound.
No kernel may reach another device: no remote copies, remote signals or barrier semaphores. Data moves between devices by JAX's collectives and lax.ppermute only.
A program may use at most 32 MiB of HBM per device.

```python
import jax
import jax.numpy as jnp

TILE = 128
F_IN = 576
F_OUT = 512
NODES = 98304


def draw_adjacency(key, part):
    key = jax.random.fold_in(key, 11)
    tile_count = NODES // TILE
    keys = jax.random.split(key, 4)
    shape = (tile_count, TILE, TILE)
    lower_hit = jax.random.randint(keys[0], shape, 0, 16) == 0
    lower_val = jax.random.randint(keys[1], shape, 1, 4)
    lower = jnp.where(lower_hit, lower_val, 0)
    not_first = (jnp.arange(tile_count) > 0)[:, None, None]
    lower = jnp.where(not_first, lower, 0)
    inner_hit = jax.random.randint(keys[2], shape, 0, 16) == 0
    inner_val = jax.random.randint(keys[3], shape, 1, 4)
    row_index = jnp.arange(TILE)[:, None]
    col_index = jnp.arange(TILE)[None, :]
    inner = jnp.where(inner_hit & (row_index < col_index)[None, :, :], inner_val, 0)
    diagonal_tile = inner + jnp.swapaxes(inner, 1, 2)
    upper = jnp.concatenate([jnp.swapaxes(lower[1:], 1, 2), jnp.zeros((1, TILE, TILE), jnp.int32)], axis=0)
    stacked = jnp.stack([lower, diagonal_tile, upper], axis=2)
    return stacked.reshape(NODES, 3 * TILE).astype(jnp.float32).astype(jnp.bfloat16)


def steps_of(rng, extent, cuts, least, largest):
    factor_of, own = 1.0, jax.random.fold_in(rng, 6)
    for position, parts in cuts:
        draws = jnp.exp(jax.random.uniform(jax.random.fold_in(own, position), (parts,), jnp.float32, least / len(cuts), largest / len(cuts)))
        factor_of = factor_of * jnp.repeat(draws, extent[position] // parts).reshape([-1 if axis == position else 1 for axis in range(len(extent))])
    return factor_of


def scatter_about(stream_key, shape, width, reach, cuts=(), held_as=jnp.bfloat16):
    result = jax.random.normal(stream_key, shape, jnp.float32) * width
    if len(cuts) > 0:
        result = steps_of(stream_key, shape, cuts, -0.22, 0.18) * result
    return jnp.clip(result, min=-reach, max=reach).astype(held_as)


def setup_inputs(seed: int = 0) -> dict:
    splits = jax.random.split(jax.random.key(seed), 7)
    return {
        "features": scatter_about(splits[0], (NODES, F_IN), 1.0, 6.0, ((0, 32), (1, 24))),
        "adjacency": draw_adjacency(jax.random.fold_in(splits[6], 71), 0),
        "w_self": scatter_about(splits[2], (F_IN, F_OUT), F_IN ** -0.5, 0.25),
        "w_neigh": scatter_about(splits[3], (F_IN, F_OUT), (F_IN // 4) ** -0.5, 0.5),
        "bias_out": scatter_about(splits[4], (F_OUT,), 0.5, 3.0, (), jnp.float32),
        "cotangent": scatter_about(splits[5], (NODES, F_OUT), 1.0, 6.0, ((0, 768),)),
    }


def band_product(band_values, values):
    tile_count = band_values.shape[0] // TILE
    columns = values.shape[1]
    padded = jnp.pad(values, ((TILE, TILE), (0, 0))).reshape(tile_count + 2, TILE, columns)
    blocks = band_values.reshape(tile_count, TILE, 3, TILE)
    summed = jnp.zeros((tile_count, TILE, columns), jnp.float32)
    for offset in range(3):
        summed = summed + jnp.einsum("tic,tcf->tif", blocks[:, :, offset, :].astype(jnp.float32), padded[offset:offset + tile_count].astype(jnp.float32))
    return summed.reshape(tile_count * TILE, columns)


def reference(features, adjacency, w_self, w_neigh, bias_out, cotangent):
    band_values = adjacency
    degree = 1.0 + jnp.sum(adjacency.astype(jnp.float32), axis=1, keepdims=True)
    means = (band_product(band_values, features) / degree).astype(jnp.bfloat16)
    preact = jnp.dot(features, w_self, preferred_element_type=jnp.float32) + jnp.dot(means, w_neigh, preferred_element_type=jnp.float32) + bias_out
    sigmoid_z = jax.nn.sigmoid(preact)
    activation = (preact * sigmoid_z).astype(jnp.bfloat16)
    grad_pre = (cotangent.astype(jnp.float32) * sigmoid_z * (1.0 + preact * (1.0 - sigmoid_z))).astype(jnp.bfloat16)
    loss_scale = NODES ** -0.5
    grad_self = jnp.dot(features.T, grad_pre, preferred_element_type=jnp.float32) * loss_scale
    grad_neigh = jnp.dot(means.T, grad_pre, preferred_element_type=jnp.float32) * loss_scale
    grad_bias = jnp.sum(grad_pre.astype(jnp.float32), axis=0) * loss_scale
    back_self = jnp.dot(grad_pre, w_self.T, preferred_element_type=jnp.float32).astype(jnp.bfloat16)
    back_means = jnp.dot(grad_pre, w_neigh.T, preferred_element_type=jnp.float32).astype(jnp.bfloat16)
    scaled_back = (back_means.astype(jnp.float32) / degree).astype(jnp.bfloat16)
    grad_feat = back_self.astype(jnp.float32) + band_product(band_values, scaled_back)
    return activation, grad_self, grad_neigh, grad_bias, grad_feat
```

```python
import jax
import jax.numpy as jnp
from jax import lax
from jax.experimental import pallas as pl
from jax.experimental.pallas import tpu as pltpu
from jax.sharding import Mesh, PartitionSpec as P

TILE = 128
BF16 = jnp.bfloat16
F32 = jnp.float32
AXES = ("y", "zh", "x", "zl", "c")
SIZES = (8, 4, 4, 3, 2)
GRAPH = ("y", "zh")
FEAT = ("x", "zl", "c")
PLANE = ("y", "x")
LINE = ("zh", "zl")
N_PLANE = 32
N_LINE = 12
N_FEAT = 24
ROWS = 72
VMEM = pl.BlockSpec(memory_space=pltpu.VMEM)
PARAMS = pltpu.CompilerParams(vmem_limit_bytes=40 * 1024 * 1024)


def dot(a, b, da, db):
    return lax.dot_general(a, b, (((da,), (db,)), ((), ())), preferred_element_type=F32)


def call(kernel, outs, n_in):
    return pl.pallas_call(
        kernel,
        out_shape=outs,
        in_specs=[VMEM] * n_in,
        out_specs=jax.tree.map(lambda _: VMEM, outs),
        compiler_params=PARAMS,
    )


def band(parts, adj):
    total = dot(parts[0], adj[:, :TILE], 1, 1)
    total += dot(parts[1], adj[:, TILE : 2 * TILE], 1, 1)
    return total + dot(parts[2], adj[:, 2 * TILE :], 1, 1)


def degrees(adj):
    return (1.0 + dot(jnp.ones((8, 3 * TILE), BF16), adj, 1, 1))[:1]


def forward_kernel(core, low, own, high, adj, ws, wn, bias, cot, act, grad, means, keep, send):
    a = adj[...]
    m = (band((low[...], own[...], high[...]), a) / degrees(a)).astype(BF16)
    means[...] = m
    x = own[...]
    pre = dot(x, ws[...], 0, 0) + dot(m, wn[...], 0, 0) + bias[...]
    s = 1.0 / (1.0 + jnp.exp(-pre))
    act[...] = (pre * s).astype(BF16)
    g = (cot[...].astype(F32) * s * (1.0 + pre * (1.0 - s))).astype(BF16)
    grad[...] = g
    first = core[0] == 0
    keep[...] = jnp.where(first, x, m)
    send[:576] = jnp.where(first, m, x)
    for b in range(4):
        send[576 + b * TILE : 576 + (b + 1) * TILE] = g[:, b * TILE : (b + 1) * TILE]


def back_kernel(grad, adj, ws, wn, back, scaled):
    g = grad[...]
    back[...] = dot(ws[...], g, 1, 1).astype(BF16)
    rounded = dot(wn[...], g, 1, 1).astype(BF16).astype(F32)
    scaled[...] = (rounded / degrees(adj[...])).astype(BF16)


def partial_kernel(keep, grad, recv, out):
    other = recv[:576]
    for b in range(4):
        g0 = grad[:, b * TILE : (b + 1) * TILE]
        g1 = recv[576 + b * TILE : 576 + (b + 1) * TILE]
        block = dot(keep[...], g0, 1, 0) + dot(other, g1, 1, 0)
        for k in range(8):
            out[b * 8 + k, :ROWS] = block[k * ROWS : (k + 1) * ROWS].astype(BF16)
    sums = [
        jnp.sum(grad[:, b * TILE : (b + 1) * TILE].astype(F32), axis=0, keepdims=True)
        + jnp.sum(recv[576 + b * TILE : 576 + (b + 1) * TILE].astype(F32), axis=0, keepdims=True)
        for b in range(4)
    ]
    tail = jnp.concatenate(sums + [jnp.zeros((4, TILE), F32)], axis=0).astype(BF16)
    for d in range(N_PLANE):
        out[d, ROWS:] = tail


def plane_kernel(recv, out):
    total = recv[0].astype(F32)
    for d in range(1, N_PLANE):
        total += recv[d].astype(F32)
    rounded = total.astype(BF16)
    for d in range(N_LINE):
        out[d] = rounded


def line_kernel(scale, recv, out, bias):
    total = recv[0].astype(F32)
    for d in range(1, N_LINE):
        total += recv[d].astype(F32)
    total *= scale
    bias[...] = total[ROWS:]
    rounded = total[:ROWS].astype(BF16)
    for d in range(N_PLANE):
        out[d] = rounded


def unpack_kernel(core, own, other, gs, gn):
    first = core[0] == 0
    for b in range(4):
        o = own[b * 576 : (b + 1) * 576].astype(F32)
        t = other[b * 576 : (b + 1) * 576].astype(F32)
        gs[:, b * TILE : (b + 1) * TILE] = jnp.where(first, o, t)
        gn[:, b * TILE : (b + 1) * TILE] = jnp.where(first, t, o)


def feat_kernel(low, own, high, adj, back, out):
    total = back[...].astype(F32) + band((low[...], own[...], high[...]), adj[...])
    out[...] = total.astype(BF16)


def split_kernel(x, out):
    for t in range(N_FEAT):
        out[t] = x[:, t * TILE : (t + 1) * TILE]


def join_kernel(x, out):
    for t in range(N_FEAT):
        out[:, t * TILE : (t + 1) * TILE] = x[t].astype(F32)


def exchange(x, axis):
    return lax.all_to_all(x, axis, split_axis=0, concat_axis=0, tiled=False)


def halos(x):
    n = 768
    low = lax.ppermute(x, AXES, [(i, i + 1) for i in range(n - 1)])
    high = lax.ppermute(x, AXES, [(i + 1, i) for i in range(n - 1)])
    return low, high


def swap(x):
    return lax.ppermute(x, "c", [(0, 1), (1, 0)])


def sds(shape, dtype=BF16):
    return jax.ShapeDtypeStruct(shape, dtype)


def local(features, adjacency, w_self, w_neigh, bias_out, cotangent):
    n_rows = features.shape[0]
    width = features.shape[1]
    f_in = width * N_FEAT
    f_out = w_self.shape[1]
    scale = (n_rows * 32) ** -0.5
    core = lax.axis_index("c").astype(jnp.int32).reshape(1)
    tile = lax.axis_index(FEAT)
    adj = lax.dynamic_slice_in_dim(adjacency, tile * TILE, TILE, axis=0)
    bias = bias_out.reshape(1, f_out)
    smem = pl.BlockSpec(memory_space=pltpu.SMEM)

    pieces = call(split_kernel, sds((N_FEAT, width, TILE)), 1)(features.T)
    own = exchange(pieces, FEAT).reshape(f_in, TILE)
    low, high = halos(own)
    act, grad, means, keep, send = pl.pallas_call(
        forward_kernel,
        out_shape=(
            sds((TILE, f_out)),
            sds((TILE, f_out)),
            sds((f_in, TILE)),
            sds((f_in, TILE)),
            sds((f_in + f_out, TILE)),
        ),
        in_specs=[smem] + [VMEM] * 8,
        out_specs=(VMEM,) * 5,
        compiler_params=PARAMS,
    )(core, low, own, high, adj, w_self, w_neigh, bias, cotangent)
    recv = swap(send)
    back, scaled = call(back_kernel, (sds((f_in, TILE)), sds((f_in, TILE))), 4)(grad, adj, w_self, w_neigh)
    partial = call(partial_kernel, sds((N_PLANE, ROWS + 8, TILE)), 3)(keep, grad, recv)
    from_plane = exchange(partial, PLANE)
    s_low, s_high = halos(scaled)
    to_line = call(plane_kernel, sds((N_LINE, ROWS + 8, TILE)), 1)(from_plane)
    from_line = exchange(to_line, LINE)
    feat_t = call(feat_kernel, sds((f_in, TILE)), 5)(s_low, scaled, s_high, adj, back)
    feat_back = exchange(feat_t.reshape(N_FEAT, width, TILE), FEAT)
    to_plane, bias_sum = call(
        lambda r, o, b: line_kernel(scale, r, o, b),
        (sds((N_PLANE, ROWS, TILE)), sds((8, TILE), F32)),
        1,
    )(from_line)
    half = exchange(to_plane, PLANE).reshape(N_PLANE * ROWS, TILE)
    other = swap(half)
    grad_self, grad_neigh = pl.pallas_call(
        unpack_kernel,
        out_shape=(sds((f_in, f_out), F32), sds((f_in, f_out), F32)),
        in_specs=[smem, VMEM, VMEM],
        out_specs=(VMEM, VMEM),
        compiler_params=PARAMS,
    )(core, half, other)
    grad_bias = bias_sum[:4].reshape(f_out)
    grad_feat = call(join_kernel, sds((width, n_rows), F32), 1)(feat_back).T
    return act, grad_self, grad_neigh, grad_bias, grad_feat


def solution(mesh):
    grid = Mesh(mesh.devices.reshape(SIZES), AXES)
    in_specs = (P(GRAPH, FEAT), P(GRAPH, None), P(), P(), P(), P(GRAPH + FEAT, None))
    out_specs = (P(GRAPH + FEAT, None), P(), P(), P(), P(GRAPH, FEAT))
    return jax.shard_map(local, mesh=grid, in_specs=in_specs, out_specs=out_specs, check_vma=False)
```

```python
import jax
import jax.numpy as jnp
from jax import lax
from jax.experimental import pallas as pl
from jax.experimental.pallas import tpu as pltpu
from jax.sharding import Mesh, PartitionSpec as P

TILE = 128
BF16 = jnp.bfloat16
F32 = jnp.float32
AXES = ("y", "zh", "x", "zl", "c")
SIZES = (8, 4, 4, 3, 2)
GRAPH = ("y", "zh")
FEAT = ("x", "zl", "c")
BLOCK = ("x", "zl")
N_BLOCK = 12
N_Y = 8
N_ZH = 4
N_FEAT = 24
ROWS = 192
TAIL = 8
SMEM = pl.BlockSpec(memory_space=pltpu.SMEM)
ANY = pl.BlockSpec(memory_space=pl.ANY)
VMEM = pl.BlockSpec(memory_space=pltpu.VMEM)
PARAMS = pltpu.CompilerParams(vmem_limit_bytes=32 * 1024 * 1024)


def dot(a, b, da, db):
    return lax.dot_general(a, b, (((da,), (db,)), ((), ())), preferred_element_type=F32)


def call(kernel, specs, outs, scratch=(), **kw):
    return pl.pallas_call(
        kernel,
        out_shape=outs,
        in_specs=list(specs),
        out_specs=kw.pop("out_specs", jax.tree.map(lambda _: VMEM, outs)),
        scratch_shapes=list(scratch),
        compiler_params=PARAMS,
        **kw,
    )


def sds(shape, dtype=BF16):
    return jax.ShapeDtypeStruct(shape, dtype)


def lanes(b):
    return slice(b * TILE, (b + 1) * TILE)


def band(parts, adj):
    total = dot(parts[0], adj[:, lanes(0)], 1, 1)
    total += dot(parts[1], adj[:, lanes(1)], 1, 1)
    return total + dot(parts[2], adj[:, lanes(2)], 1, 1)


def prepare_kernel(tile, feats, adjacency, out, adj, held, sems):
    rows = pl.ds(pl.multiple_of(tile[0] * TILE, TILE), TILE)
    copies = (
        pltpu.make_async_copy(feats, held, sems.at[0]),
        pltpu.make_async_copy(adjacency.at[rows], adj, sems.at[1]),
    )
    for c in copies:
        c.start()
    copies[0].wait()
    for t in range(N_FEAT):
        out[t] = held[:, lanes(t)]
    copies[1].wait()


def forward_kernel(
    core, low, own, high, adj, ws_hbm, wn_hbm, bias_hbm, cot_hbm,
    act, grad, keep, send, back, scaled,
    ws, wn, bias, cot, sems,
):
    pairs = ((ws_hbm, ws), (wn_hbm, wn), (bias_hbm, bias), (cot_hbm, cot))
    copies = [pltpu.make_async_copy(s, d, sems.at[i]) for i, (s, d) in enumerate(pairs)]
    for c in copies:
        c.start()
    a = adj[...]
    degree = (1.0 + dot(jnp.ones((8, 3 * TILE), BF16), a, 1, 1))[:1]
    m = (band((low[...], own[...], high[...]), a) / degree).astype(BF16)
    x = own[...]
    for c in copies:
        c.wait()
    pre = dot(x, ws[...], 0, 0) + dot(m, wn[...], 0, 0) + bias[...]
    s = 1.0 / (1.0 + jnp.exp(-pre))
    act[...] = (pre * s).astype(BF16)
    g = (cot[...].astype(F32) * s * (1.0 + pre * (1.0 - s))).astype(BF16)
    grad[...] = g
    first = core[0] == 0
    keep[...] = jnp.where(first, x, m)
    send[:576] = jnp.where(first, m, x)
    for b in range(4):
        send[576 + b * TILE : 576 + (b + 1) * TILE] = g[:, lanes(b)]
    back[...] = dot(ws[...], g, 1, 1).astype(BF16)
    rounded = dot(wn[...], g, 1, 1).astype(BF16).astype(F32)
    scaled[...] = (rounded / degree).astype(BF16)


def partial_kernel(keep, grad, recv, out):
    other = recv[:576]
    sums = []
    for b in range(4):
        g0 = grad[:, lanes(b)]
        g1 = recv[576 + b * TILE : 576 + (b + 1) * TILE]
        block = dot(keep[...], g0, 1, 0) + dot(other, g1, 1, 0)
        for k in range(3):
            out[b * 3 + k, :ROWS] = block[k * ROWS : (k + 1) * ROWS].astype(BF16)
        sums.append(
            jnp.sum(g0.astype(F32), axis=0, keepdims=True)
            + jnp.sum(g1.astype(F32), axis=0, keepdims=True)
        )
    tail = jnp.concatenate(sums + [jnp.zeros((TAIL - 4, TILE), F32)], axis=0).astype(BF16)
    for d in range(N_BLOCK):
        out[d, ROWS:] = tail


def sum_kernel(recv, out):
    total = recv[0].astype(F32)
    for d in range(1, recv.shape[0]):
        total += recv[d].astype(F32)
    rounded = total.astype(BF16)
    for d in range(out.shape[0]):
        out[d] = rounded


def last_sum_kernel(scale, core, recv, keep, other, out, bias):
    total = recv[0].astype(F32)
    for d in range(1, N_ZH):
        total += recv[d].astype(F32)
    total *= scale
    bias[...] = total[ROWS:]
    rounded = total[:ROWS].astype(BF16)
    first = core[0] == 0
    for d in range(N_BLOCK):
        out[d, :ROWS] = rounded
        k = keep[d].astype(F32)
        o = other[d].astype(F32)
        pair = jnp.concatenate([jnp.where(first, k, o), jnp.where(first, o, k)], axis=0)
        out[d, ROWS:] = pair.astype(BF16)


def halves(block, held):
    for d in range(N_BLOCK):
        rows = slice((d % 3) * ROWS, (d % 3 + 1) * ROWS)
        held[rows, lanes(d // 3)] = block[d, :ROWS].astype(F32)


def own_kernel(core, block, gs, gn, gf, held, sem):
    halves(block, held)
    first = core[0] == 0

    @pl.when(first)
    def _():
        pltpu.make_async_copy(held, gs, sem).start()

    @pl.when(jnp.logical_not(first))
    def _():
        pltpu.make_async_copy(held, gn, sem).start()

    width = gf.shape[0]
    for d in range(N_BLOCK):
        pair = block[d, ROWS:].astype(F32)
        gf[:, lanes(2 * d)] = pair[:width]
        gf[:, lanes(2 * d + 1)] = pair[width:]
    pltpu.make_async_copy(held, gs, sem).wait()


def other_kernel(core, block, gs_in, gn_in, gs, gn, held, sem):
    halves(block, held)
    first = core[0] == 0

    @pl.when(first)
    def _():
        pltpu.make_async_copy(held, gn, sem).start()

    @pl.when(jnp.logical_not(first))
    def _():
        pltpu.make_async_copy(held, gs, sem).start()

    pltpu.make_async_copy(held, gs, sem).wait()


def feat_kernel(core, low, own, high, adj, back, keep, send):
    total = back[...].astype(F32) + band((low[...], own[...], high[...]), adj[...])
    first = core[0] == 0
    width = total.shape[0] // N_FEAT
    for d in range(N_BLOCK):
        even = total[2 * d * width : (2 * d + 1) * width]
        odd = total[(2 * d + 1) * width : (2 * d + 2) * width]
        keep[d] = jnp.where(first, even, odd).astype(BF16)
        send[d] = jnp.where(first, odd, even).astype(BF16)


def exchange(x, axis):
    return lax.all_to_all(x, axis, split_axis=0, concat_axis=0, tiled=False)


def halos(x):
    n = 768
    low = lax.ppermute(x, AXES, [(i, i + 1) for i in range(n - 1)])
    high = lax.ppermute(x, AXES, [(i + 1, i) for i in range(n - 1)])
    return low, high


def swap(x):
    return lax.ppermute(x, "c", [(0, 1), (1, 0)])


def local(features, adjacency, w_self, w_neigh, bias_out, cotangent):
    n_rows, width = features.shape
    f_in, f_out = w_self.shape
    scale = (n_rows * 32) ** -0.5
    core = lax.axis_index("c").astype(jnp.int32).reshape(1)
    tile = lax.axis_index(FEAT).astype(jnp.int32).reshape(1)
    dma = pltpu.SemaphoreType.DMA
    wide = sds((f_in, TILE))
    weight = sds((f_in, f_out), F32)

    pieces, adj = call(
        prepare_kernel,
        [SMEM, ANY, ANY],
        (sds((N_FEAT, width, TILE)), sds((TILE, 3 * TILE))),
        [pltpu.VMEM((width, n_rows), BF16), dma((2,))],
    )(tile, features.T, adjacency)
    own = exchange(pieces, FEAT).reshape(f_in, TILE)
    low, high = halos(own)
    act, grad, keep, send, back, scaled = call(
        forward_kernel,
        [SMEM] + [VMEM] * 4 + [ANY] * 4,
        (sds((TILE, f_out)), sds((TILE, f_out)), wide, sds((f_in + f_out, TILE)), wide, wide),
        [
            pltpu.VMEM((f_in, f_out), BF16),
            pltpu.VMEM((f_in, f_out), BF16),
            pltpu.VMEM((1, f_out), F32),
            pltpu.VMEM((TILE, f_out), BF16),
            dma((4,)),
        ],
    )(core, low, own, high, adj, w_self, w_neigh, bias_out.reshape(1, f_out), cotangent)
    recv = swap(send)
    s_low, s_high = halos(scaled)
    partial = call(partial_kernel, [VMEM] * 3, sds((N_BLOCK, ROWS + TAIL, TILE)))(keep, grad, recv)
    from_block = exchange(partial, BLOCK)
    slab = sds((N_BLOCK, width, TILE))
    from_block, s_low, s_high = lax.optimization_barrier((from_block, s_low, s_high))
    f_keep, f_send = call(feat_kernel, [SMEM] + [VMEM] * 5, (slab, slab))(
        core, s_low, scaled, s_high, adj, back
    )
    f_recv = swap(f_send)
    from_y = exchange(call(sum_kernel, [VMEM], sds((N_Y, ROWS + TAIL, TILE)))(from_block), "y")
    from_y, f_recv = lax.optimization_barrier((from_y, f_recv))
    from_zh = exchange(call(sum_kernel, [VMEM], sds((N_ZH, ROWS + TAIL, TILE)))(from_y), "zh")
    to_block, bias_sum = call(
        lambda *refs: last_sum_kernel(scale, *refs),
        [SMEM] + [VMEM] * 3,
        (sds((N_BLOCK, ROWS + 2 * width, TILE)), sds((TAIL, TILE), F32)),
    )(core, from_zh, f_keep, f_recv)
    block = exchange(to_block, BLOCK)
    other = swap(block)
    held = [pltpu.VMEM((f_in, f_out), F32), dma]
    gs, gn, gf = call(
        own_kernel,
        [SMEM, VMEM],
        (weight, weight, sds((width, n_rows), F32)),
        held,
        out_specs=(ANY, ANY, VMEM),
    )(core, block)
    grad_self, grad_neigh = call(
        other_kernel,
        [SMEM, VMEM, ANY, ANY],
        (weight, weight),
        held,
        out_specs=(ANY, ANY),
        input_output_aliases={2: 0, 3: 1},
    )(core, other, gs, gn)
    return act, grad_self, grad_neigh, bias_sum[:4].reshape(f_out), gf.T


def solution(mesh):
    grid = Mesh(mesh.devices.reshape(SIZES), AXES)
    in_specs = (P(GRAPH, FEAT), P(GRAPH, None), P(), P(), P(), P(GRAPH + FEAT, None))
    out_specs = (P(GRAPH + FEAT, None), P(), P(), P(), P(GRAPH, FEAT))
    return jax.shard_map(local, mesh=grid, in_specs=in_specs, out_specs=out_specs, check_vma=False)
```

```python
import jax
import jax.numpy as jnp
from jax import lax
from jax.experimental import pallas as pl
from jax.experimental.pallas import tpu as pltpu
from jax.sharding import Mesh, PartitionSpec as P

TILE = 128
BF16 = jnp.bfloat16
F32 = jnp.float32
AXES = ("y", "zh", "x", "zl", "c")
SIZES = (8, 4, 4, 3, 2)
GRAPH = ("y", "zh")
FEAT = ("x", "zl", "c")
LINE = ("zh", "zl")
N_X = 4
N_Y = 8
N_LINE = 12
N_FEAT = 24
ROWS = 72
TAIL = 8
SMEM = pl.BlockSpec(memory_space=pltpu.SMEM)
ANY = pl.BlockSpec(memory_space=pl.ANY)
VMEM = pl.BlockSpec(memory_space=pltpu.VMEM)
PARAMS = pltpu.CompilerParams(vmem_limit_bytes=32 * 1024 * 1024)


def dot(a, b, da, db):
    return lax.dot_general(a, b, (((da,), (db,)), ((), ())), preferred_element_type=F32)


def call(kernel, specs, outs, scratch=(), **kw):
    return pl.pallas_call(
        kernel,
        out_shape=outs,
        in_specs=list(specs),
        out_specs=kw.pop("out_specs", jax.tree.map(lambda _: VMEM, outs)),
        scratch_shapes=list(scratch),
        compiler_params=kw.pop("params", PARAMS),
        **kw,
    )


def sds(shape, dtype=BF16):
    return jax.ShapeDtypeStruct(shape, dtype)


def lanes(b):
    return slice(b * TILE, (b + 1) * TILE)


def band(parts, adj):
    return dot(jnp.concatenate(parts, axis=1), adj, 1, 1)


def prepare_kernel(feats, out):
    for t in range(N_FEAT):
        out[t] = feats[:, lanes(t)]


def load_kernel(tile, adjacency, *refs):
    rows = pl.ds(pl.multiple_of(tile[0] * TILE, TILE), TILE)
    sems = refs[-1]
    sources = (adjacency.at[rows],) + refs[:4]
    copies = [
        pltpu.make_async_copy(s, d, sems.at[i])
        for i, (s, d) in enumerate(zip(sources, refs[4:-1], strict=True))
    ]
    for c in copies:
        c.start()
    for c in copies:
        c.wait()


def forward_kernel(
    core, low, own, high, adj, ws, wn, bias, cot, act, grad, keep, send, back, scaled
):
    a = adj[...]
    degree = (1.0 + dot(jnp.ones((8, 3 * TILE), BF16), a, 1, 1))[:1]
    m = (band((low[...], own[...], high[...]), a) / degree).astype(BF16)
    x = own[...]
    pre = dot(x, ws[...], 0, 0) + dot(m, wn[...], 0, 0) + bias[...]
    s = 1.0 / (1.0 + jnp.exp(-pre))
    act[...] = (pre * s).astype(BF16)
    g = (cot[...].astype(F32) * s * (1.0 + pre * (1.0 - s))).astype(BF16)
    grad[...] = g
    first = core[0] == 0
    keep[...] = jnp.where(first, x, m)
    send[:576] = jnp.where(first, m, x)
    for b in range(4):
        send[576 + b * TILE : 576 + (b + 1) * TILE] = g[:, lanes(b)]
    back[...] = dot(ws[...], g, 1, 1).astype(BF16)
    rounded = dot(wn[...], g, 1, 1).astype(BF16).astype(F32)
    scaled[...] = (rounded / degree).astype(BF16)


def partial_kernel(keep, grad, recv, out):
    f_in = keep.shape[0]
    rows = [recv[f_in + b * TILE : f_in + (b + 1) * TILE] for b in range(N_X)]
    g = jnp.concatenate([grad[...], jnp.concatenate(rows, axis=1)], axis=0)
    total = dot(jnp.concatenate([keep[...], recv[:f_in]], axis=1), g, 1, 0)
    sums = jnp.sum(g.astype(F32), axis=0, keepdims=True)
    parts = [sums[:, lanes(b)] for b in range(N_X)]
    tail = jnp.concatenate(parts + [jnp.zeros((TAIL - N_X, TILE), F32)], axis=0)
    for b in range(N_X):
        out[b] = jnp.concatenate([total[:, lanes(b)], tail], axis=0).astype(BF16)


def summed(recv):
    total = recv[0].astype(F32)
    for d in range(1, recv.shape[0]):
        total += recv[d].astype(F32)
    return total


def x_kernel(recv, out):
    total = summed(recv)
    tail = total[N_Y * ROWS :]
    for d in range(N_Y):
        out[d] = jnp.concatenate([total[d * ROWS : (d + 1) * ROWS], tail], axis=0).astype(BF16)


def y_kernel(recv, out):
    rounded = summed(recv).astype(BF16)
    for d in range(N_LINE):
        out[d] = rounded


def line_kernel(scale, recv, out, bias):
    total = summed(recv) * scale
    bias[...] = jnp.concatenate([total[ROWS + b : ROWS + b + 1] for b in range(N_X)], axis=1)
    rounded = total[:ROWS].astype(BF16)
    for d in range(N_Y):
        out[d] = rounded


def feat_kernel(core, low, own, high, adj, back, keep, send):
    total = back[...].astype(F32) + band((low[...], own[...], high[...]), adj[...])
    first = core[0] == 0
    width = total.shape[0] // N_FEAT
    for d in range(N_LINE):
        even = total[2 * d * width : (2 * d + 1) * width]
        odd = total[(2 * d + 1) * width : (2 * d + 2) * width]
        keep[d % 3, d // 3] = jnp.where(first, even, odd).astype(BF16)
        send[d % 3, d // 3] = jnp.where(first, odd, even).astype(BF16)


def pair_kernel(core, zl, keep, other, stay, up, down):
    first = core[0] == 0
    for shift, out in enumerate((stay, up, down)):
        at = lax.rem(zl[0] + shift, 3)
        for d in range(N_X):
            k = keep[at, d].astype(F32)
            o = other[at, d].astype(F32)
            pair = jnp.concatenate([jnp.where(first, k, o), jnp.where(first, o, k)], axis=0)
            out[d] = pair.astype(BF16)


def join_kernel(zl, grads, stay, low, high, out):
    f_in = grads.shape[0]
    pair = stay.shape[1]
    whole = grads[...]
    place = zl[0]
    for d in range(N_X):
        out[d, :f_in] = whole
        for p in range(3):
            far = jnp.where(place == (p + 1) % 3, low[d], high[d])
            out[d, f_in + p * pair : f_in + (p + 1) * pair] = jnp.where(place == p, stay[d], far)


def halves(block, held, copies):
    for d in range(N_X):
        held[:, lanes(d)] = block[d, : held.shape[0]].astype(F32)
        copies(d)


def send_half(held, sems, first, yes, no):
    def copies(d):
        @pl.when(first)
        def _():
            pltpu.make_async_copy(held.at[:, lanes(d)], yes.at[:, lanes(d)], sems.at[d]).start()

        @pl.when(jnp.logical_not(first))
        def _():
            pltpu.make_async_copy(held.at[:, lanes(d)], no.at[:, lanes(d)], sems.at[d]).start()

    return copies


def finish(held, sems, out):
    for d in range(N_X):
        pltpu.make_async_copy(held.at[:, lanes(d)], out.at[:, lanes(d)], sems.at[d]).wait()


def own_kernel(core, block, gs, gn, gf, held, sems):
    halves(block, held, send_half(held, sems, core[0] == 0, gs, gn))
    f_in = held.shape[0]
    width = gf.shape[0]
    for d in range(N_X):
        part = block[d, f_in:].astype(F32)
        for k in range(6):
            gf[:, lanes(6 * d + k)] = part[k * width : (k + 1) * width]
    finish(held, sems, gs)


def other_kernel(core, block, gs_in, gn_in, gs, gn, held, sems):
    halves(block, held, send_half(held, sems, core[0] == 0, gn, gs))
    finish(held, sems, gs)


def exchange(x, axis):
    return lax.all_to_all(x, axis, split_axis=0, concat_axis=0, tiled=False)


def halos(x):
    n = 768
    low = lax.ppermute(x, AXES, [(i, i + 1) for i in range(n - 1)])
    high = lax.ppermute(x, AXES, [(i + 1, i) for i in range(n - 1)])
    return low, high


def swap(x):
    return lax.ppermute(x, "c", [(0, 1), (1, 0)])


def local(features, adjacency, w_self, w_neigh, bias_out, cotangent):
    n_rows, width = features.shape
    f_in, f_out = w_self.shape
    scale = (n_rows * 32) ** -0.5
    core = lax.axis_index("c").astype(jnp.int32).reshape(1)
    tile = lax.axis_index(FEAT).astype(jnp.int32).reshape(1)
    dma = pltpu.SemaphoreType.DMA
    wide = sds((f_in, TILE))
    weight = sds((f_in, f_out), F32)

    pieces = call(prepare_kernel, [VMEM], sds((N_FEAT, width, TILE)))(features.T)
    own = exchange(pieces, FEAT).reshape(f_in, TILE)
    held = call(
        load_kernel,
        [SMEM] + [ANY] * 5,
        (
            sds((TILE, 3 * TILE)),
            sds((f_in, f_out)),
            sds((f_in, f_out)),
            sds((1, f_out), F32),
            sds((TILE, f_out)),
        ),
        [dma((5,))],
        params=pltpu.CompilerParams(vmem_limit_bytes=52 * 1024 * 1024),
    )(tile, adjacency, w_self, w_neigh, bias_out.reshape(1, f_out), cotangent)
    own, held = lax.optimization_barrier((own, held))
    adj = held[0]
    low, high = halos(own)
    act, grad, keep, send, back, scaled = call(
        forward_kernel,
        [SMEM] + [VMEM] * 8,
        (sds((TILE, f_out)), sds((TILE, f_out)), wide, sds((f_in + f_out, TILE)), wide, wide),
    )(core, low, own, high, *held)
    recv = swap(send)
    s_low, s_high = halos(scaled)
    partial = call(partial_kernel, [VMEM] * 3, sds((N_X, f_in + TAIL, TILE)))(keep, grad, recv)
    from_x = exchange(partial, "x")
    from_x, s_low, s_high = lax.optimization_barrier((from_x, s_low, s_high))
    from_y = exchange(call(x_kernel, [VMEM], sds((N_Y, ROWS + TAIL, TILE)))(from_x), "y")
    slab = sds((3, N_X, width, TILE))
    f_keep, f_send = call(feat_kernel, [SMEM] + [VMEM] * 5, (slab, slab))(
        core, s_low, scaled, s_high, adj, back
    )
    f_recv = swap(f_send)
    from_y, f_recv = lax.optimization_barrier((from_y, f_recv))
    from_line = exchange(call(y_kernel, [VMEM], sds((N_LINE, ROWS + TAIL, TILE)))(from_y), LINE)
    zl = lax.axis_index("zl").astype(jnp.int32).reshape(1)
    pair = sds((N_X, 2 * width, TILE))
    stay, up, down = call(pair_kernel, [SMEM] * 2 + [VMEM] * 2, (pair,) * 3)(core, zl, f_keep, f_recv)
    f_low = lax.ppermute(up, "zl", [(i, (i + 1) % 3) for i in range(3)])
    f_high = lax.ppermute(down, "zl", [(i, (i + 2) % 3) for i in range(3)])
    from_line, f_low, f_high = lax.optimization_barrier((from_line, f_low, f_high))
    to_y, bias_sum = call(
        lambda *refs: line_kernel(scale, *refs),
        [VMEM],
        (sds((N_Y, ROWS, TILE)), sds((1, f_out), F32)),
    )(from_line)
    column = exchange(to_y, "y").reshape(f_in, TILE)
    to_x = call(join_kernel, [SMEM] + [VMEM] * 4, sds((N_X, f_in + 6 * width, TILE)))(
        zl, column, stay, f_low, f_high
    )
    block = exchange(to_x, "x")
    other = swap(block)
    held = [pltpu.VMEM((f_in, f_out), F32), dma((N_X,))]
    gs, gn, gf = call(
        own_kernel,
        [SMEM, VMEM],
        (weight, weight, sds((width, n_rows), F32)),
        held,
        out_specs=(ANY, ANY, VMEM),
    )(core, block)
    grad_self, grad_neigh = call(
        other_kernel,
        [SMEM, VMEM, ANY, ANY],
        (weight, weight),
        held,
        out_specs=(ANY, ANY),
        input_output_aliases={2: 0, 3: 1},
    )(core, other, gs, gn)
    return act, grad_self, grad_neigh, bias_sum.reshape(f_out), gf.T


def solution(mesh):
    grid = Mesh(mesh.devices.reshape(SIZES), AXES)
    in_specs = (P(GRAPH, FEAT), P(GRAPH, None), P(), P(), P(), P(GRAPH + FEAT, None))
    out_specs = (P(GRAPH + FEAT, None), P(), P(), P(), P(GRAPH, FEAT))
    return jax.shard_map(local, mesh=grid, in_specs=in_specs, out_specs=out_specs, check_vma=False)
```

```python
import jax
import jax.numpy as jnp
from jax import lax
from jax.experimental import pallas as pl
from jax.experimental.pallas import tpu as pltpu
from jax.sharding import Mesh, PartitionSpec as P

TILE = 128
BF16 = jnp.bfloat16
F32 = jnp.float32
AXES = ("y", "zh", "x", "zl", "c")
SIZES = (8, 4, 4, 3, 2)
GRAPH = ("y", "zh")
FEAT = ("x", "zl", "c")
LINE = ("zh", "zl")
N_X = 4
N_Y = 8
N_LINE = 12
N_FEAT = 24
ROWS = 72
TAIL = 8
SMEM = pl.BlockSpec(memory_space=pltpu.SMEM)
ANY = pl.BlockSpec(memory_space=pl.ANY)
VMEM = pl.BlockSpec(memory_space=pltpu.VMEM)
PARAMS = pltpu.CompilerParams(vmem_limit_bytes=32 * 1024 * 1024)


def dot(a, b, da, db):
    return lax.dot_general(a, b, (((da,), (db,)), ((), ())), preferred_element_type=F32)


def call(kernel, specs, outs, scratch=(), **kw):
    return pl.pallas_call(
        kernel,
        out_shape=outs,
        in_specs=list(specs),
        out_specs=kw.pop("out_specs", jax.tree.map(lambda _: VMEM, outs)),
        scratch_shapes=list(scratch),
        compiler_params=PARAMS,
        **kw,
    )


def sds(shape, dtype=BF16):
    return jax.ShapeDtypeStruct(shape, dtype)


def lanes(b):
    return slice(b * TILE, (b + 1) * TILE)


def band(parts, adj):
    return dot(jnp.concatenate(parts, axis=1), adj, 1, 1)


def prepare_kernel(tile, feats, adjacency, *refs):
    held, sems = refs[-2:]
    rows = pl.ds(pl.multiple_of(tile[0] * TILE, TILE), TILE)
    pairs = [(feats, held), (adjacency.at[rows], refs[5])]
    pairs += [(refs[i], refs[i + 6]) for i in range(4)]
    out = refs[4]
    copies = [pltpu.make_async_copy(s, d, sems.at[i]) for i, (s, d) in enumerate(pairs)]
    for c in copies:
        c.start()
    copies[0].wait()
    for t in range(N_FEAT):
        out[t] = held[:, lanes(t)]
    for c in copies[1:]:
        c.wait()


def sides(core, far, near):
    first = core[0] == 0
    f, n = far[...], near[...]
    return jnp.where(first, f, n), jnp.where(first, n, f)


def forward_kernel(
    core, near, far, own, adj, ws, wn, bias, cot, act, grad, keep, send, back, scaled
):
    a = adj[...]
    degree = (1.0 + dot(jnp.ones((8, 3 * TILE), BF16), a, 1, 1))[:1]
    low, high = sides(core, far, near)
    m = (band((low, own[...], high), a) / degree).astype(BF16)
    x = own[...]
    pre = dot(x, ws[...], 0, 0) + dot(m, wn[...], 0, 0) + bias[...]
    s = 1.0 / (1.0 + jnp.exp(-pre))
    act[...] = (pre * s).astype(BF16)
    g = (cot[...].astype(F32) * s * (1.0 + pre * (1.0 - s))).astype(BF16)
    grad[...] = g
    first = core[0] == 0
    keep[...] = jnp.where(first, x, m)
    send[:576] = jnp.where(first, m, x)
    for b in range(4):
        send[576 + b * TILE : 576 + (b + 1) * TILE] = g[:, lanes(b)]
    back[...] = dot(ws[...], g, 1, 1).astype(BF16)
    rounded = dot(wn[...], g, 1, 1).astype(BF16).astype(F32)
    scaled[...] = (rounded / degree).astype(BF16)


def partial_kernel(keep, grad, recv, out):
    f_in = keep.shape[0]
    rows = [recv[f_in + b * TILE : f_in + (b + 1) * TILE] for b in range(N_X)]
    g = jnp.concatenate([grad[...], jnp.concatenate(rows, axis=1)], axis=0)
    total = dot(jnp.concatenate([keep[...], recv[:f_in]], axis=1), g, 1, 0)
    sums = jnp.sum(g.astype(F32), axis=0, keepdims=True)
    parts = [sums[:, lanes(b)] for b in range(N_X)]
    tail = jnp.concatenate(parts + [jnp.zeros((TAIL - N_X, TILE), F32)], axis=0)
    for b in range(N_X):
        out[b] = jnp.concatenate([total[:, lanes(b)], tail], axis=0).astype(BF16)


def summed(recv):
    total = recv[0].astype(F32)
    for d in range(1, recv.shape[0]):
        total += recv[d].astype(F32)
    return total


def x_kernel(recv, out):
    total = summed(recv)
    tail = total[N_Y * ROWS :]
    for d in range(N_Y):
        out[d] = jnp.concatenate([total[d * ROWS : (d + 1) * ROWS], tail], axis=0).astype(BF16)


def y_kernel(recv, out):
    rounded = summed(recv).astype(BF16)
    for d in range(N_LINE):
        out[d] = rounded


def line_kernel(scale, recv, out, bias):
    total = summed(recv) * scale
    bias[...] = jnp.concatenate([total[ROWS + b : ROWS + b + 1] for b in range(N_X)], axis=1)
    rounded = total[:ROWS].astype(BF16)
    for d in range(N_Y):
        out[d] = rounded


def feat_kernel(core, zl, near, far, own, adj, back, stay, up, down, parts):
    low, high = sides(core, far, near)
    total = back[...].astype(F32) + band((low, own[...], high), adj[...])
    width = parts.shape[1]
    for i in range(N_FEAT):
        parts[i] = total[i * width : (i + 1) * width]
    for shift, out in enumerate((stay, up, down)):
        at = 2 * lax.rem(zl[0] + shift, 3)
        for d in range(N_X):
            pair = jnp.concatenate([parts[6 * d + at], parts[6 * d + at + 1]], axis=0)
            out[d] = pair.astype(BF16)


def join_kernel(zl, grads, stay, low, high, out):
    f_in = grads.shape[0]
    pair = stay.shape[1]
    whole = grads[...]
    place = zl[0]
    for d in range(N_X):
        out[d, :f_in] = whole
        for p in range(3):
            far = jnp.where(place == (p + 1) % 3, low[d], high[d])
            out[d, f_in + p * pair : f_in + (p + 1) * pair] = jnp.where(place == p, stay[d], far)


def halves(block, held, copies):
    for d in range(N_X):
        held[:, lanes(d)] = block[d, : held.shape[0]].astype(F32)
        copies(d)


def send_half(held, sems, first, yes, no):
    def copies(d):
        @pl.when(first)
        def _():
            pltpu.make_async_copy(held.at[:, lanes(d)], yes.at[:, lanes(d)], sems.at[d]).start()

        @pl.when(jnp.logical_not(first))
        def _():
            pltpu.make_async_copy(held.at[:, lanes(d)], no.at[:, lanes(d)], sems.at[d]).start()

    return copies


def finish(held, sems, out):
    for d in range(N_X):
        pltpu.make_async_copy(held.at[:, lanes(d)], out.at[:, lanes(d)], sems.at[d]).wait()


def columns(core, source, block, gf, part, sems):
    width = part.shape[1]
    f_in = block.shape[1] - 6 * width
    first = core == 0
    copies = []
    for d in range(N_X):
        rows = block[d, f_in:].astype(F32)
        for p in range(3):
            k = 3 * d + p
            even = rows[2 * p * width : (2 * p + 1) * width]
            odd = rows[(2 * p + 1) * width : (2 * p + 2) * width]
            at = pl.ds(pl.multiple_of((2 * k + source) * TILE, TILE), TILE)
            part[k] = jnp.where(first, even, odd)
            copies.append(pltpu.make_async_copy(part.at[k], gf.at[:, at], sems.at[k]))
            copies[-1].start()
    return copies


def own_kernel(core, block, gs, gn, gf, held, sems, part, part_sems):
    halves(block, held, send_half(held, sems, core[0] == 0, gs, gn))
    copies = columns(core[0], core[0], block, gf, part, part_sems)
    finish(held, sems, gs)
    for c in copies:
        c.wait()


def other_kernel(core, block, gs_in, gn_in, gf_in, gs, gn, gf, held, sems, part, part_sems):
    halves(block, held, send_half(held, sems, core[0] == 0, gn, gs))
    copies = columns(core[0], 1 - core[0], block, gf, part, part_sems)
    finish(held, sems, gs)
    for c in copies:
        c.wait()


def exchange(x, axis):
    return lax.all_to_all(x, axis, split_axis=0, concat_axis=0, tiled=False)


def halos(x):
    pairs = [(2 * k + 1, 2 * k + 2) for k in range(383)]
    pairs += [(b, a) for a, b in pairs]
    near = swap(x)
    return lax.ppermute(x, AXES, pairs), near


def swap(x):
    return lax.ppermute(x, "c", [(0, 1), (1, 0)])


def local(features, adjacency, w_self, w_neigh, bias_out, cotangent):
    n_rows, width = features.shape
    f_in, f_out = w_self.shape
    scale = (n_rows * 32) ** -0.5
    core = lax.axis_index("c").astype(jnp.int32).reshape(1)
    tile = lax.axis_index(FEAT).astype(jnp.int32).reshape(1)
    dma = pltpu.SemaphoreType.DMA
    wide = sds((f_in, TILE))
    weight = sds((f_in, f_out), F32)

    pieces, *held = call(
        prepare_kernel,
        [SMEM] + [ANY] * 6,
        (
            sds((N_FEAT, width, TILE)),
            sds((TILE, 3 * TILE)),
            sds((f_in, f_out)),
            sds((f_in, f_out)),
            sds((1, f_out), F32),
            sds((TILE, f_out)),
        ),
        [pltpu.VMEM((width, n_rows), BF16), dma((6,))],
    )(
        tile,
        *(
            pltpu.with_memory_space_constraint(x, pltpu.HBM)
            for x in (features.T, adjacency, w_self, w_neigh, bias_out.reshape(1, f_out), cotangent)
        ),
    )
    adj = held[0]
    own = exchange(pieces, FEAT).reshape(f_in, TILE)
    far, near = halos(own)
    act, grad, keep, send, back, scaled = call(
        forward_kernel,
        [SMEM] + [VMEM] * 8,
        (sds((TILE, f_out)), sds((TILE, f_out)), wide, sds((f_in + f_out, TILE)), wide, wide),
    )(core, near, far, own, *held)
    recv = swap(send)
    s_far, s_near = halos(scaled)
    partial = call(partial_kernel, [VMEM] * 3, sds((N_X, f_in + TAIL, TILE)))(keep, grad, recv)
    from_x = exchange(partial, "x")
    from_x, s_far, s_near = lax.optimization_barrier((from_x, s_far, s_near))
    zl = lax.axis_index("zl").astype(jnp.int32).reshape(1)
    pair = sds((N_X, 2 * width, TILE))
    stay, up, down = call(
        feat_kernel,
        [SMEM] * 2 + [VMEM] * 5,
        (pair,) * 3,
        [pltpu.VMEM((N_FEAT, width, TILE), F32)],
    )(core, zl, s_near, s_far, scaled, adj, back)
    from_x, stay, up, down = lax.optimization_barrier((from_x, stay, up, down))
    from_y = exchange(call(x_kernel, [VMEM], sds((N_Y, ROWS + TAIL, TILE)))(from_x), "y")
    from_line = exchange(call(y_kernel, [VMEM], sds((N_LINE, ROWS + TAIL, TILE)))(from_y), LINE)
    f_low = lax.ppermute(up, "zl", [(i, (i + 1) % 3) for i in range(3)])
    f_high = lax.ppermute(down, "zl", [(i, (i + 2) % 3) for i in range(3)])
    from_line, f_low, f_high = lax.optimization_barrier((from_line, f_low, f_high))
    to_y, bias_sum = call(
        lambda *refs: line_kernel(scale, *refs),
        [VMEM],
        (sds((N_Y, ROWS, TILE)), sds((1, f_out), F32)),
    )(from_line)
    column = exchange(to_y, "y").reshape(f_in, TILE)
    to_x = call(join_kernel, [SMEM] + [VMEM] * 4, sds((N_X, f_in + 6 * width, TILE)))(
        zl, column, stay, f_low, f_high
    )
    block = exchange(to_x, "x")
    other = swap(block)
    whole = sds((width, n_rows), F32)
    room = [
        pltpu.VMEM((f_in, f_out), F32),
        dma((N_X,)),
        pltpu.VMEM((N_LINE, width, TILE), F32),
        dma((N_LINE,)),
    ]
    partly = call(
        own_kernel, [SMEM, VMEM], (weight, weight, whole), room, out_specs=(ANY,) * 3
    )(core, block)
    grad_self, grad_neigh, gf = call(
        other_kernel,
        [SMEM, VMEM] + [ANY] * 3,
        (weight, weight, whole),
        room,
        out_specs=(ANY,) * 3,
        input_output_aliases={2: 0, 3: 1, 4: 2},
    )(core, other, *partly)
    return act, grad_self, grad_neigh, bias_sum.reshape(f_out), gf.T


def solution(mesh):
    grid = Mesh(mesh.devices.reshape(SIZES), AXES)
    in_specs = (P(GRAPH, FEAT), P(GRAPH, None), P(), P(), P(), P(GRAPH + FEAT, None))
    out_specs = (P(GRAPH + FEAT, None), P(), P(), P(), P(GRAPH, FEAT))
    return jax.shard_map(local, mesh=grid, in_specs=in_specs, out_specs=out_specs, check_vma=False)
```

```python
import jax
import jax.numpy as jnp
from jax import lax
from jax.experimental import pallas as pl
from jax.experimental.pallas import tpu as pltpu
from jax.sharding import Mesh, PartitionSpec as P

TILE = 128
BF16 = jnp.bfloat16
F32 = jnp.float32
AXES = ("y", "zh", "x", "zl", "c")
SIZES = (8, 4, 4, 3, 2)
GRAPH = ("y", "zh")
FEAT = ("x", "zl", "c")
LINE = ("zh", "zl")
N_X = 4
N_Y = 8
N_LINE = 12
N_FEAT = 24
ROWS = 72
TAIL = 8
SMEM = pl.BlockSpec(memory_space=pltpu.SMEM)
ANY = pl.BlockSpec(memory_space=pl.ANY)
VMEM = pl.BlockSpec(memory_space=pltpu.VMEM)
PARAMS = pltpu.CompilerParams(vmem_limit_bytes=32 * 1024 * 1024)


def dot(a, b, da, db):
    return lax.dot_general(a, b, (((da,), (db,)), ((), ())), preferred_element_type=F32)


def call(kernel, specs, outs, scratch=(), **kw):
    return pl.pallas_call(
        kernel,
        out_shape=outs,
        in_specs=list(specs),
        out_specs=kw.pop("out_specs", jax.tree.map(lambda _: VMEM, outs)),
        scratch_shapes=list(scratch),
        compiler_params=PARAMS,
        **kw,
    )


def sds(shape, dtype=BF16):
    return jax.ShapeDtypeStruct(shape, dtype)


def lanes(b):
    return slice(b * TILE, (b + 1) * TILE)


def band(parts, adj):
    return dot(jnp.concatenate(parts, axis=1), adj, 1, 1)


def prepare_kernel(tile, feats, adjacency, *refs):
    held, sems = refs[-2:]
    rows = pl.ds(pl.multiple_of(tile[0] * TILE, TILE), TILE)
    pairs = [(feats, held), (adjacency.at[rows], refs[5])]
    pairs += [(refs[i], refs[i + 6]) for i in range(4)]
    out = refs[4]
    copies = [pltpu.make_async_copy(s, d, sems.at[i]) for i, (s, d) in enumerate(pairs)]
    for c in copies:
        c.start()
    copies[0].wait()
    for t in range(N_FEAT):
        out[t] = held[:, lanes(t)]
    for c in copies[1:]:
        c.wait()


def sides(core, far, near):
    first = core[0] == 0
    f, n = far[...], near[...]
    return jnp.where(first, f, n), jnp.where(first, n, f)


def forward_kernel(
    core, near, far, own, adj, ws, wn, bias, cot, act, grad, keep, send, back, scaled
):
    a = adj[...]
    degree = (1.0 + dot(jnp.ones((8, 3 * TILE), BF16), a, 1, 1))[:1]
    low, high = sides(core, far, near)
    m = (band((low, own[...], high), a) / degree).astype(BF16)
    x = own[...]
    pre = dot(x, ws[...], 0, 0) + dot(m, wn[...], 0, 0) + bias[...]
    s = 1.0 / (1.0 + jnp.exp(-pre))
    act[...] = (pre * s).astype(BF16)
    g = (cot[...].astype(F32) * s * (1.0 + pre * (1.0 - s))).astype(BF16)
    grad[...] = g
    first = core[0] == 0
    keep[...] = jnp.where(first, x, m)
    send[:576] = jnp.where(first, m, x)
    for b in range(4):
        send[576 + b * TILE : 576 + (b + 1) * TILE] = g[:, lanes(b)]
    back[...] = dot(ws[...], g, 1, 1).astype(BF16)
    rounded = dot(wn[...], g, 1, 1).astype(BF16).astype(F32)
    scaled[...] = (rounded / degree).astype(BF16)


def partial_kernel(keep, grad, recv, out):
    f_in = keep.shape[0]
    rows = [recv[f_in + b * TILE : f_in + (b + 1) * TILE] for b in range(N_X)]
    g = jnp.concatenate([grad[...], jnp.concatenate(rows, axis=1)], axis=0)
    total = dot(jnp.concatenate([keep[...], recv[:f_in]], axis=1), g, 1, 0)
    sums = jnp.sum(g.astype(F32), axis=0, keepdims=True)
    parts = [sums[:, lanes(b)] for b in range(N_X)]
    tail = jnp.concatenate(parts + [jnp.zeros((TAIL - N_X, TILE), F32)], axis=0)
    for b in range(N_X):
        out[b] = jnp.concatenate([total[:, lanes(b)], tail], axis=0).astype(BF16)


def summed(recv):
    total = recv[0].astype(F32)
    for d in range(1, recv.shape[0]):
        total += recv[d].astype(F32)
    return total


def x_kernel(recv, out):
    total = summed(recv)
    tail = total[N_Y * ROWS :]
    for d in range(N_Y):
        out[d] = jnp.concatenate([total[d * ROWS : (d + 1) * ROWS], tail], axis=0).astype(BF16)


def y_kernel(recv, out):
    rounded = summed(recv).astype(BF16)
    for d in range(N_LINE):
        out[d] = rounded


def line_kernel(scale, recv, out, bias):
    total = summed(recv) * scale
    bias[...] = jnp.concatenate([total[ROWS + b : ROWS + b + 1] for b in range(N_X)], axis=1)
    rounded = total[:ROWS].astype(BF16)
    for d in range(N_Y):
        out[d] = rounded


def feat_kernel(core, zl, near, far, own, adj, back, stay, up, down, parts):
    low, high = sides(core, far, near)
    total = back[...].astype(F32) + band((low, own[...], high), adj[...])
    width = parts.shape[1]
    for i in range(N_FEAT):
        parts[i] = total[i * width : (i + 1) * width]
    for shift, out in enumerate((stay, up, down)):
        at = 2 * lax.rem(zl[0] + shift, 3)
        for d in range(N_X):
            pair = jnp.concatenate([parts[6 * d + at], parts[6 * d + at + 1]], axis=0)
            out[d] = pair.astype(BF16)


def join_kernel(zl, grads, stay, low, high, out):
    f_in = grads.shape[0]
    pair = stay.shape[1]
    whole = grads[...]
    place = zl[0]
    for d in range(N_X):
        out[d, :f_in] = whole
        for p in range(3):
            far = jnp.where(place == (p + 1) % 3, low[d], high[d])
            out[d, f_in + p * pair : f_in + (p + 1) * pair] = jnp.where(place == p, stay[d], far)


def halves(block, held, copies):
    for d in range(N_X):
        held[:, lanes(d)] = block[d, : held.shape[0]].astype(F32)
        copies(d)


def send_half(held, sems, first, yes, no):
    def copies(d):
        @pl.when(first)
        def _():
            pltpu.make_async_copy(held.at[:, lanes(d)], yes.at[:, lanes(d)], sems.at[d]).start()

        @pl.when(jnp.logical_not(first))
        def _():
            pltpu.make_async_copy(held.at[:, lanes(d)], no.at[:, lanes(d)], sems.at[d]).start()

    return copies


def finish(held, sems, out):
    for d in range(N_X):
        pltpu.make_async_copy(held.at[:, lanes(d)], out.at[:, lanes(d)], sems.at[d]).wait()


def columns(core, source, block, gf, part, sems):
    width = part.shape[1]
    f_in = block.shape[1] - 6 * width
    first = core == 0
    copies = []
    for d in range(N_X):
        rows = block[d, f_in:].astype(F32)
        for p in range(3):
            k = 3 * d + p
            even = rows[2 * p * width : (2 * p + 1) * width]
            odd = rows[(2 * p + 1) * width : (2 * p + 2) * width]
            at = pl.ds(pl.multiple_of((2 * k + source) * TILE, TILE), TILE)
            part[k] = jnp.where(first, even, odd)
            copies.append(pltpu.make_async_copy(part.at[k], gf.at[:, at], sems.at[k]))
            copies[-1].start()
    return copies


def own_kernel(core, block, gs, gn, gf, held, sems, part, part_sems):
    halves(block, held, send_half(held, sems, core[0] == 0, gs, gn))
    copies = columns(core[0], core[0], block, gf, part, part_sems)
    finish(held, sems, gs)
    for c in copies:
        c.wait()


def other_kernel(core, block, gs_in, gn_in, gf_in, gs, gn, gf, held, sems, part, part_sems):
    halves(block, held, send_half(held, sems, core[0] == 0, gn, gs))
    copies = columns(core[0], 1 - core[0], block, gf, part, part_sems)
    finish(held, sems, gs)
    for c in copies:
        c.wait()


def exchange(x, axis):
    return lax.all_to_all(x, axis, split_axis=0, concat_axis=0, tiled=False)


def halos(x):
    pairs = [(2 * k + 1, 2 * k + 2) for k in range(383)]
    pairs += [(b, a) for a, b in pairs]
    near = swap(x)
    return lax.ppermute(x, AXES, pairs), near


def swap(x):
    return lax.ppermute(x, "c", [(0, 1), (1, 0)])


def local(features, adjacency, w_self, w_neigh, bias_out, cotangent):
    n_rows, width = features.shape
    f_in, f_out = w_self.shape
    scale = (n_rows * 32) ** -0.5
    core = lax.axis_index("c").astype(jnp.int32).reshape(1)
    tile = lax.axis_index(FEAT).astype(jnp.int32).reshape(1)
    dma = pltpu.SemaphoreType.DMA
    wide = sds((f_in, TILE))
    weight = sds((f_in, f_out), F32)

    pieces, *held = call(
        prepare_kernel,
        [SMEM] + [ANY] * 6,
        (
            sds((N_FEAT, width, TILE)),
            sds((TILE, 3 * TILE)),
            sds((f_in, f_out)),
            sds((f_in, f_out)),
            sds((1, f_out), F32),
            sds((TILE, f_out)),
        ),
        [pltpu.VMEM((width, n_rows), BF16), dma((6,))],
    )(
        tile,
        *(
            pltpu.with_memory_space_constraint(x, pltpu.HBM)
            for x in (features.T, adjacency, w_self, w_neigh, bias_out.reshape(1, f_out), cotangent)
        ),
    )
    adj = held[0]
    own = exchange(pieces, FEAT).reshape(f_in, TILE)
    far, near = halos(own)
    act, grad, keep, send, back, scaled = call(
        forward_kernel,
        [SMEM] + [VMEM] * 8,
        (sds((TILE, f_out)), sds((TILE, f_out)), wide, sds((f_in + f_out, TILE)), wide, wide),
    )(core, near, far, own, *held)
    recv = swap(send)
    s_far, s_near = halos(scaled)
    partial = call(partial_kernel, [VMEM] * 3, sds((N_X, f_in + TAIL, TILE)))(keep, grad, recv)
    from_x = exchange(partial, "x")
    from_y = exchange(call(x_kernel, [VMEM], sds((N_Y, ROWS + TAIL, TILE)))(from_x), "y")
    from_y, s_far, s_near = lax.optimization_barrier((from_y, s_far, s_near))
    zl = lax.axis_index("zl").astype(jnp.int32).reshape(1)
    pair = sds((N_X, 2 * width, TILE))
    stay, up, down = call(
        feat_kernel,
        [SMEM] * 2 + [VMEM] * 5,
        (pair,) * 3,
        [pltpu.VMEM((N_FEAT, width, TILE), F32)],
    )(core, zl, s_near, s_far, scaled, adj, back)
    from_y, stay, up, down = lax.optimization_barrier((from_y, stay, up, down))
    from_line = exchange(call(y_kernel, [VMEM], sds((N_LINE, ROWS + TAIL, TILE)))(from_y), LINE)
    f_low = lax.ppermute(up, "zl", [(i, (i + 1) % 3) for i in range(3)])
    f_high = lax.ppermute(down, "zl", [(i, (i + 2) % 3) for i in range(3)])
    to_y, bias_sum = call(
        lambda *refs: line_kernel(scale, *refs),
        [VMEM],
        (sds((N_Y, ROWS, TILE)), sds((1, f_out), F32)),
    )(from_line)
    column = exchange(to_y, "y").reshape(f_in, TILE)
    to_x = call(join_kernel, [SMEM] + [VMEM] * 4, sds((N_X, f_in + 6 * width, TILE)))(
        zl, column, stay, f_low, f_high
    )
    block = exchange(to_x, "x")
    other = swap(block)
    whole = sds((width, n_rows), F32)
    room = [
        pltpu.VMEM((f_in, f_out), F32),
        dma((N_X,)),
        pltpu.VMEM((N_LINE, width, TILE), F32),
        dma((N_LINE,)),
    ]
    partly = call(
        own_kernel, [SMEM, VMEM], (weight, weight, whole), room, out_specs=(ANY,) * 3
    )(core, block)
    grad_self, grad_neigh, gf = call(
        other_kernel,
        [SMEM, VMEM] + [ANY] * 3,
        (weight, weight, whole),
        room,
        out_specs=(ANY,) * 3,
        input_output_aliases={2: 0, 3: 1, 4: 2},
    )(core, other, *partly)
    return act, grad_self, grad_neigh, bias_sum.reshape(f_out), gf.T


def solution(mesh):
    grid = Mesh(mesh.devices.reshape(SIZES), AXES)
    in_specs = (P(GRAPH, FEAT), P(GRAPH, None), P(), P(), P(), P(GRAPH + FEAT, None))
    out_specs = (P(GRAPH + FEAT, None), P(), P(), P(), P(GRAPH, FEAT))
    return jax.shard_map(local, mesh=grid, in_specs=in_specs, out_specs=out_specs, check_vma=False)
```

```python
import jax
import jax.numpy as jnp
from jax import lax
from jax.experimental import pallas as pl
from jax.experimental.pallas import tpu as pltpu
from jax.sharding import Mesh, PartitionSpec as P

TILE = 128
BF16 = jnp.bfloat16
F32 = jnp.float32
AXES = ("y", "zh", "x", "zl", "c")
SIZES = (8, 4, 4, 3, 2)
GRAPH = ("y", "zh")
FEAT = ("x", "zl", "c")
LINE = ("zh", "zl")
N_X = 4
N_Y = 8
N_LINE = 12
N_FEAT = 24
ROWS = 72
TAIL = 8
SMEM = pl.BlockSpec(memory_space=pltpu.SMEM)
ANY = pl.BlockSpec(memory_space=pl.ANY)
VMEM = pl.BlockSpec(memory_space=pltpu.VMEM)
PARAMS = pltpu.CompilerParams(vmem_limit_bytes=32 * 1024 * 1024)


def dot(a, b, da, db):
    return lax.dot_general(a, b, (((da,), (db,)), ((), ())), preferred_element_type=F32)


def call(kernel, specs, outs, scratch=(), **kw):
    return pl.pallas_call(
        kernel,
        out_shape=outs,
        in_specs=list(specs),
        out_specs=kw.pop("out_specs", jax.tree.map(lambda _: VMEM, outs)),
        scratch_shapes=list(scratch),
        compiler_params=PARAMS,
        **kw,
    )


def sds(shape, dtype=BF16):
    return jax.ShapeDtypeStruct(shape, dtype)


def lanes(b):
    return slice(b * TILE, (b + 1) * TILE)


def band(parts, adj):
    return dot(jnp.concatenate(parts, axis=1), adj, 1, 1)


def prepare_kernel(feats, out, held, sem):
    copy = pltpu.make_async_copy(feats, held, sem)
    copy.start()
    copy.wait()
    for t in range(N_FEAT):
        out[t] = held[:, lanes(t)]


def load_kernel(tile, adjacency, *refs):
    rows = pl.ds(pl.multiple_of(tile[0] * TILE, TILE), TILE)
    sources, targets, sems = (adjacency.at[rows],) + refs[:4], refs[4:-1], refs[-1]
    copies = [
        pltpu.make_async_copy(s, d, sems.at[i])
        for i, (s, d) in enumerate(zip(sources, targets, strict=True))
    ]
    for c in copies:
        c.start()
    for c in copies:
        c.wait()


def sides(core, f, n):
    first = core[0] == 0
    return jnp.where(first, f, n), jnp.where(first, n, f)


def forward_kernel(
    core, near, far, own, adj, ws, wn, bias, cot, act, grad, keep, send, back, scaled
):
    a = adj[...]
    degree = (1.0 + dot(jnp.ones((8, 3 * TILE), BF16), a, 1, 1))[:1]
    low, high = sides(core, far[...], near[...])
    m = (band((low, own[...], high), a) / degree).astype(BF16)
    x = own[...]
    pre = dot(x, ws[...], 0, 0) + dot(m, wn[...], 0, 0) + bias[...]
    s = 1.0 / (1.0 + jnp.exp(-pre))
    act[...] = (pre * s).astype(BF16)
    g = (cot[...].astype(F32) * s * (1.0 + pre * (1.0 - s))).astype(BF16)
    grad[...] = g
    first = core[0] == 0
    keep[...] = jnp.where(first, x, m)
    send[:576] = jnp.where(first, m, x)
    for b in range(4):
        send[576 + b * TILE : 576 + (b + 1) * TILE] = g[:, lanes(b)]
    back[...] = dot(ws[...], g, 1, 1).astype(BF16)
    rounded = dot(wn[...], g, 1, 1).astype(BF16).astype(F32)
    scale = (rounded / degree).astype(BF16)
    scaled[...] = scale
    send[576 + 4 * TILE :] = scale


def partial_kernel(keep, grad, recv, act, out, act_out):
    act_out[...] = act[...]
    f_in = keep.shape[0]
    rows = [recv[f_in + b * TILE : f_in + (b + 1) * TILE] for b in range(N_X)]
    g = jnp.concatenate([grad[...], jnp.concatenate(rows, axis=1)], axis=0)
    total = dot(jnp.concatenate([keep[...], recv[:f_in]], axis=1), g, 1, 0)
    sums = jnp.sum(g.astype(F32), axis=0, keepdims=True)
    parts = [sums[:, lanes(b)] for b in range(N_X)]
    tail = jnp.concatenate(parts + [jnp.zeros((TAIL - N_X, TILE), F32)], axis=0)
    for b in range(N_X):
        out[b] = jnp.concatenate([total[:, lanes(b)], tail], axis=0).astype(BF16)


def summed(recv):
    total = recv[0].astype(F32)
    for d in range(1, recv.shape[0]):
        total += recv[d].astype(F32)
    return total


def x_kernel(recv, out):
    total = summed(recv)
    tail = total[N_Y * ROWS :]
    for d in range(N_Y):
        out[d] = jnp.concatenate([total[d * ROWS : (d + 1) * ROWS], tail], axis=0).astype(BF16)


def y_kernel(recv, out):
    rounded = summed(recv).astype(BF16)
    for d in range(N_LINE):
        out[d] = rounded


def line_kernel(scale, recv, out, bias):
    total = summed(recv) * scale
    bias[...] = jnp.concatenate([total[ROWS + b : ROWS + b + 1] for b in range(N_X)], axis=1)
    rounded = total[:ROWS].astype(BF16)
    for d in range(N_Y):
        out[d] = rounded


def feat_kernel(core, zl, recv, far, own, adj, back, stay, up, down, parts):
    low, high = sides(core, far[...], recv[recv.shape[0] - own.shape[0] :])
    total = back[...].astype(F32) + band((low, own[...], high), adj[...])
    width = parts.shape[1]
    for i in range(N_FEAT):
        parts[i] = total[i * width : (i + 1) * width]
    for shift, out in enumerate((stay, up, down)):
        at = 2 * lax.rem(zl[0] + shift, 3)
        for d in range(N_X):
            pair = jnp.concatenate([parts[6 * d + at], parts[6 * d + at + 1]], axis=0)
            out[d] = pair.astype(BF16)


def join_kernel(zl, grads, stay, low, high, out):
    f_in = grads.shape[0]
    pair = stay.shape[1]
    whole = grads[...]
    place = zl[0]
    for d in range(N_X):
        out[d, :f_in] = whole
        for p in range(3):
            far = jnp.where(place == (p + 1) % 3, low[d], high[d])
            out[d, f_in + p * pair : f_in + (p + 1) * pair] = jnp.where(place == p, stay[d], far)


def halves(block, held, copies):
    for d in range(N_X):
        held[:, lanes(d)] = block[d, : held.shape[0]].astype(F32)
        copies(d)


def send_half(held, sems, first, yes, no):
    def copies(d):
        @pl.when(first)
        def _():
            pltpu.make_async_copy(held.at[:, lanes(d)], yes.at[:, lanes(d)], sems.at[d]).start()

        @pl.when(jnp.logical_not(first))
        def _():
            pltpu.make_async_copy(held.at[:, lanes(d)], no.at[:, lanes(d)], sems.at[d]).start()

    return copies


def finish(held, sems, out):
    for d in range(N_X):
        pltpu.make_async_copy(held.at[:, lanes(d)], out.at[:, lanes(d)], sems.at[d]).wait()


def columns(core, source, block, gf, part, sems):
    width = part.shape[1]
    f_in = block.shape[1] - 6 * width
    first = core == 0
    copies = []
    for d in range(N_X):
        rows = block[d, f_in:].astype(F32)
        for p in range(3):
            k = 3 * d + p
            even = rows[2 * p * width : (2 * p + 1) * width]
            odd = rows[(2 * p + 1) * width : (2 * p + 2) * width]
            at = pl.ds(pl.multiple_of((2 * k + source) * TILE, TILE), TILE)
            part[k] = jnp.where(first, even, odd)
            copies.append(pltpu.make_async_copy(part.at[k], gf.at[:, at], sems.at[k]))
            copies[-1].start()
    return copies


def own_kernel(core, block, gs, gn, gf, held, sems, part, part_sems):
    halves(block, held, send_half(held, sems, core[0] == 0, gs, gn))
    copies = columns(core[0], core[0], block, gf, part, part_sems)
    finish(held, sems, gs)
    for c in copies:
        c.wait()


def other_kernel(core, block, gs_in, gn_in, gf_in, gs, gn, gf, held, sems, part, part_sems):
    halves(block, held, send_half(held, sems, core[0] == 0, gn, gs))
    copies = columns(core[0], 1 - core[0], block, gf, part, part_sems)
    finish(held, sems, gs)
    for c in copies:
        c.wait()


def exchange(x, axis):
    return lax.all_to_all(x, axis, split_axis=0, concat_axis=0, tiled=False)


def across(x):
    pairs = [(2 * k + 1, 2 * k + 2) for k in range(383)]
    pairs += [(b, a) for a, b in pairs]
    return lax.ppermute(x, AXES, pairs)

def swap(x):
    return lax.ppermute(x, "c", [(0, 1), (1, 0)])


def local(features, adjacency, w_self, w_neigh, bias_out, cotangent):
    n_rows, width = features.shape
    f_in, f_out = w_self.shape
    scale = (n_rows * 32) ** -0.5
    core = lax.axis_index("c").astype(jnp.int32).reshape(1)
    tile = lax.axis_index(FEAT).astype(jnp.int32).reshape(1)
    dma = pltpu.SemaphoreType.DMA
    wide = sds((f_in, TILE))
    weight = sds((f_in, f_out), F32)

    def pinned(x):
        return pltpu.with_memory_space_constraint(x, pltpu.HBM)

    pieces = call(
        prepare_kernel, [ANY], sds((N_FEAT, width, TILE)), [pltpu.VMEM((width, n_rows), BF16), dma]
    )(pinned(features.T))
    own = exchange(pieces, FEAT).reshape(f_in, TILE)
    near, far = swap(own), across(own)
    held = call(
        load_kernel,
        [SMEM] + [ANY] * 5,
        (
            sds((TILE, 3 * TILE)),
            sds((f_in, f_out)),
            sds((f_in, f_out)),
            sds((1, f_out), F32),
            sds((TILE, f_out)),
        ),
        [dma((5,))],
    )(tile, *map(pinned, (adjacency, w_self, w_neigh, bias_out.reshape(1, f_out), cotangent)))
    near, far, held = lax.optimization_barrier((near, far, held))
    adj = held[0]
    act, grad, keep, send, back, scaled = call(
        forward_kernel,
        [SMEM] + [VMEM] * 8,
        (sds((TILE, f_out)), sds((TILE, f_out)), wide, sds((2 * f_in + f_out, TILE)), wide, wide),
    )(core, near, far, own, *held)
    recv = swap(send)
    s_far = across(scaled)
    partial, act = call(
        partial_kernel, [VMEM] * 4, (sds((N_X, f_in + TAIL, TILE)), sds((TILE, f_out)))
    )(keep, grad, recv, act)
    from_x = exchange(partial, "x")
    from_x, s_far = lax.optimization_barrier((from_x, s_far))
    zl = lax.axis_index("zl").astype(jnp.int32).reshape(1)
    pair = sds((N_X, 2 * width, TILE))
    stay, up, down = call(
        feat_kernel,
        [SMEM] * 2 + [VMEM] * 5,
        (pair,) * 3,
        [pltpu.VMEM((N_FEAT, width, TILE), F32)],
    )(core, zl, recv, s_far, scaled, adj, back)
    from_x, stay, up, down = lax.optimization_barrier((from_x, stay, up, down))
    from_y = exchange(call(x_kernel, [VMEM], sds((N_Y, ROWS + TAIL, TILE)))(from_x), "y")
    from_line = exchange(call(y_kernel, [VMEM], sds((N_LINE, ROWS + TAIL, TILE)))(from_y), LINE)
    f_low = lax.ppermute(up, "zl", [(i, (i + 1) % 3) for i in range(3)])
    f_high = lax.ppermute(down, "zl", [(i, (i + 2) % 3) for i in range(3)])
    from_line, f_low, f_high = lax.optimization_barrier((from_line, f_low, f_high))
    to_y, bias_sum = call(
        lambda *refs: line_kernel(scale, *refs),
        [VMEM],
        (sds((N_Y, ROWS, TILE)), sds((1, f_out), F32)),
    )(from_line)
    column = exchange(to_y, "y").reshape(f_in, TILE)
    to_x = call(join_kernel, [SMEM] + [VMEM] * 4, sds((N_X, f_in + 6 * width, TILE)))(
        zl, column, stay, f_low, f_high
    )
    block = exchange(to_x, "x")
    other = swap(block)
    whole = sds((width, n_rows), F32)
    room = [
        pltpu.VMEM((f_in, f_out), F32),
        dma((N_X,)),
        pltpu.VMEM((N_LINE, width, TILE), F32),
        dma((N_LINE,)),
    ]
    partly = call(
        own_kernel, [SMEM, VMEM], (weight, weight, whole), room, out_specs=(ANY,) * 3
    )(core, block)
    grad_self, grad_neigh, gf = call(
        other_kernel,
        [SMEM, VMEM] + [ANY] * 3,
        (weight, weight, whole),
        room,
        out_specs=(ANY,) * 3,
        input_output_aliases={2: 0, 3: 1, 4: 2},
    )(core, other, *partly)
    return act, grad_self, grad_neigh, bias_sum.reshape(f_out), gf.T


def solution(mesh):
    grid = Mesh(mesh.devices.reshape(SIZES), AXES)
    in_specs = (P(GRAPH, FEAT), P(GRAPH, None), P(), P(), P(), P(GRAPH + FEAT, None))
    out_specs = (P(GRAPH + FEAT, None), P(), P(), P(), P(GRAPH, FEAT))
    return jax.shard_map(local, mesh=grid, in_specs=in_specs, out_specs=out_specs, check_vma=False)
```

```python
import jax
import jax.numpy as jnp
from jax import lax
from jax.experimental import pallas as pl
from jax.experimental.pallas import tpu as pltpu
from jax.sharding import Mesh, PartitionSpec as P

TILE = 128
BF16 = jnp.bfloat16
F32 = jnp.float32
AXES = ("y", "zh", "x", "zl", "c")
SIZES = (8, 4, 4, 3, 2)
GRAPH = ("y", "zh")
FEAT = ("x", "zl", "c")
PLANE = ("y", "x")
LINE = ("zh", "zl")
N_X = 4
N_Y = 8
N_LINE = 12
N_FEAT = 24
ROWS = 72
TAIL = 8
SMEM = pl.BlockSpec(memory_space=pltpu.SMEM)
ANY = pl.BlockSpec(memory_space=pl.ANY)
VMEM = pl.BlockSpec(memory_space=pltpu.VMEM)
PARAMS = pltpu.CompilerParams(vmem_limit_bytes=32 * 1024 * 1024)


def dot(a, b, da, db):
    return lax.dot_general(a, b, (((da,), (db,)), ((), ())), preferred_element_type=F32)


def call(kernel, specs, outs, scratch=(), **kw):
    return pl.pallas_call(
        kernel,
        out_shape=outs,
        in_specs=list(specs),
        out_specs=kw.pop("out_specs", jax.tree.map(lambda _: VMEM, outs)),
        scratch_shapes=list(scratch),
        compiler_params=PARAMS,
        **kw,
    )


def sds(shape, dtype=BF16):
    return jax.ShapeDtypeStruct(shape, dtype)


def lanes(b):
    return slice(b * TILE, (b + 1) * TILE)


def band(parts, adj):
    return dot(jnp.concatenate(parts, axis=1), adj, 1, 1)


def prepare_kernel(feats, out, held, sem):
    copy = pltpu.make_async_copy(feats, held, sem)
    copy.start()
    copy.wait()
    for t in range(N_FEAT):
        out[t] = held[:, lanes(t)]


def load_kernel(tile, adjacency, *refs):
    rows = pl.ds(pl.multiple_of(tile[0] * TILE, TILE), TILE)
    sources, targets, sems = (adjacency.at[rows],) + refs[:4], refs[4:-1], refs[-1]
    copies = [
        pltpu.make_async_copy(s, d, sems.at[i])
        for i, (s, d) in enumerate(zip(sources, targets, strict=True))
    ]
    for c in copies:
        c.start()
    for c in copies:
        c.wait()


def sides(core, f, n):
    first = core[0] == 0
    return jnp.where(first, f, n), jnp.where(first, n, f)


def forward_kernel(
    core, near, far, own, adj, ws, wn, bias, cot, act, grad, keep, send, back, scaled
):
    a = adj[...]
    degree = (1.0 + dot(jnp.ones((8, 3 * TILE), BF16), a, 1, 1))[:1]
    low, high = sides(core, far[...], near[...])
    m = (band((low, own[...], high), a) / degree).astype(BF16)
    x = own[...]
    pre = dot(x, ws[...], 0, 0) + dot(m, wn[...], 0, 0) + bias[...]
    s = 1.0 / (1.0 + jnp.exp(-pre))
    act[...] = (pre * s).astype(BF16)
    g = (cot[...].astype(F32) * s * (1.0 + pre * (1.0 - s))).astype(BF16)
    grad[...] = g
    first = core[0] == 0
    keep[...] = jnp.where(first, x, m)
    send[:576] = jnp.where(first, m, x)
    for b in range(4):
        send[576 + b * TILE : 576 + (b + 1) * TILE] = g[:, lanes(b)]
    back[...] = dot(ws[...], g, 1, 1).astype(BF16)
    rounded = dot(wn[...], g, 1, 1).astype(BF16).astype(F32)
    scale = (rounded / degree).astype(BF16)
    scaled[...] = scale
    send[576 + 4 * TILE :] = scale


def partial_kernel(keep, grad, recv, act, out, act_out):
    act_out[...] = act[...]
    f_in = keep.shape[0]
    rows = [recv[f_in + b * TILE : f_in + (b + 1) * TILE] for b in range(N_X)]
    g = jnp.concatenate([grad[...], jnp.concatenate(rows, axis=1)], axis=0)
    total = dot(jnp.concatenate([keep[...], recv[:f_in]], axis=1), g, 1, 0)
    sums = jnp.sum(g.astype(F32), axis=0, keepdims=True)
    parts = [sums[:, lanes(b)] for b in range(N_X)]
    tail = jnp.concatenate(parts + [jnp.zeros((TAIL - N_X, TILE), F32)], axis=0)
    for y in range(N_Y):
        for x in range(N_X):
            piece = total[y * ROWS : (y + 1) * ROWS, lanes(x)]
            out[y * N_X + x] = jnp.concatenate([piece, tail], axis=0).astype(BF16)


def summed(recv):
    total = recv[0].astype(F32)
    for d in range(1, recv.shape[0]):
        total += recv[d].astype(F32)
    return total


def plane_kernel(recv, out):
    rounded = summed(recv).astype(BF16)
    for d in range(N_LINE):
        out[d] = rounded


def line_kernel(scale, recv, out, bias):
    total = summed(recv) * scale
    bias[...] = jnp.concatenate([total[ROWS + b : ROWS + b + 1] for b in range(N_X)], axis=1)
    rounded = total[:ROWS].astype(BF16)
    for d in range(N_Y):
        out[d] = rounded


def feat_kernel(core, zl, recv, far, own, adj, back, stay, up, down, parts):
    low, high = sides(core, far[...], recv[recv.shape[0] - own.shape[0] :])
    total = back[...].astype(F32) + band((low, own[...], high), adj[...])
    width = parts.shape[1]
    for i in range(N_FEAT):
        parts[i] = total[i * width : (i + 1) * width]
    for shift, out in enumerate((stay, up, down)):
        at = 2 * lax.rem(zl[0] + shift, 3)
        for d in range(N_X):
            pair = jnp.concatenate([parts[6 * d + at], parts[6 * d + at + 1]], axis=0)
            out[d] = pair.astype(BF16)


def join_kernel(zl, grads, stay, low, high, out):
    f_in = grads.shape[0]
    pair = stay.shape[1]
    whole = grads[...]
    place = zl[0]
    for d in range(N_X):
        out[d, :f_in] = whole
        for p in range(3):
            far = jnp.where(place == (p + 1) % 3, low[d], high[d])
            out[d, f_in + p * pair : f_in + (p + 1) * pair] = jnp.where(place == p, stay[d], far)


def halves(block, held, copies):
    for d in range(N_X):
        held[:, lanes(d)] = block[d, : held.shape[0]].astype(F32)
        copies(d)


def send_half(held, sems, first, yes, no):
    def copies(d):
        @pl.when(first)
        def _():
            pltpu.make_async_copy(held.at[:, lanes(d)], yes.at[:, lanes(d)], sems.at[d]).start()

        @pl.when(jnp.logical_not(first))
        def _():
            pltpu.make_async_copy(held.at[:, lanes(d)], no.at[:, lanes(d)], sems.at[d]).start()

    return copies


def finish(held, sems, out):
    for d in range(N_X):
        pltpu.make_async_copy(held.at[:, lanes(d)], out.at[:, lanes(d)], sems.at[d]).wait()


def columns(core, source, block, gf, part, sems):
    width = part.shape[1]
    f_in = block.shape[1] - 6 * width
    first = core == 0
    copies = []
    for d in range(N_X):
        rows = block[d, f_in:].astype(F32)
        for p in range(3):
            k = 3 * d + p
            even = rows[2 * p * width : (2 * p + 1) * width]
            odd = rows[(2 * p + 1) * width : (2 * p + 2) * width]
            at = pl.ds(pl.multiple_of((2 * k + source) * TILE, TILE), TILE)
            part[k] = jnp.where(first, even, odd)
            copies.append(pltpu.make_async_copy(part.at[k], gf.at[:, at], sems.at[k]))
            copies[-1].start()
    return copies


def own_kernel(core, block, gs, gn, gf, held, sems, part, part_sems):
    halves(block, held, send_half(held, sems, core[0] == 0, gs, gn))
    copies = columns(core[0], core[0], block, gf, part, part_sems)
    finish(held, sems, gs)
    for c in copies:
        c.wait()


def other_kernel(core, block, gs_in, gn_in, gf_in, gs, gn, gf, held, sems, part, part_sems):
    halves(block, held, send_half(held, sems, core[0] == 0, gn, gs))
    copies = columns(core[0], 1 - core[0], block, gf, part, part_sems)
    finish(held, sems, gs)
    for c in copies:
        c.wait()


def exchange(x, axis):
    return lax.all_to_all(x, axis, split_axis=0, concat_axis=0, tiled=False)


def across(x):
    pairs = [(2 * k + 1, 2 * k + 2) for k in range(383)]
    pairs += [(b, a) for a, b in pairs]
    return lax.ppermute(x, AXES, pairs)

def swap(x):
    return lax.ppermute(x, "c", [(0, 1), (1, 0)])


def local(features, adjacency, w_self, w_neigh, bias_out, cotangent):
    n_rows, width = features.shape
    f_in, f_out = w_self.shape
    scale = (n_rows * 32) ** -0.5
    core = lax.axis_index("c").astype(jnp.int32).reshape(1)
    tile = lax.axis_index(FEAT).astype(jnp.int32).reshape(1)
    dma = pltpu.SemaphoreType.DMA
    wide = sds((f_in, TILE))
    weight = sds((f_in, f_out), F32)

    def pinned(x):
        return pltpu.with_memory_space_constraint(x, pltpu.HBM)

    pieces = call(
        prepare_kernel, [ANY], sds((N_FEAT, width, TILE)), [pltpu.VMEM((width, n_rows), BF16), dma]
    )(pinned(features.T))
    own = exchange(pieces, FEAT).reshape(f_in, TILE)
    near, far = swap(own), across(own)
    held = call(
        load_kernel,
        [SMEM] + [ANY] * 5,
        (
            sds((TILE, 3 * TILE)),
            sds((f_in, f_out)),
            sds((f_in, f_out)),
            sds((1, f_out), F32),
            sds((TILE, f_out)),
        ),
        [dma((5,))],
    )(tile, *map(pinned, (adjacency, w_self, w_neigh, bias_out.reshape(1, f_out), cotangent)))
    near, far, held = lax.optimization_barrier((near, far, held))
    adj = held[0]
    act, grad, keep, send, back, scaled = call(
        forward_kernel,
        [SMEM] + [VMEM] * 8,
        (sds((TILE, f_out)), sds((TILE, f_out)), wide, sds((2 * f_in + f_out, TILE)), wide, wide),
    )(core, near, far, own, *held)
    recv = swap(send)
    s_far = across(scaled)
    partial, act = call(
        partial_kernel, [VMEM] * 4, (sds((N_Y * N_X, ROWS + TAIL, TILE)), sds((TILE, f_out)))
    )(keep, grad, recv, act)
    from_plane = exchange(partial, PLANE)
    zl = lax.axis_index("zl").astype(jnp.int32).reshape(1)
    pair = sds((N_X, 2 * width, TILE))
    stay, up, down = call(
        feat_kernel,
        [SMEM] * 2 + [VMEM] * 5,
        (pair,) * 3,
        [pltpu.VMEM((N_FEAT, width, TILE), F32)],
    )(core, zl, recv, s_far, scaled, adj, back)
    f_low = lax.ppermute(up, "zl", [(i, (i + 1) % 3) for i in range(3)])
    f_high = lax.ppermute(down, "zl", [(i, (i + 2) % 3) for i in range(3)])
    from_plane, f_low, f_high = lax.optimization_barrier((from_plane, f_low, f_high))
    to_line = call(plane_kernel, [VMEM], sds((N_LINE, ROWS + TAIL, TILE)))(from_plane)
    from_line = exchange(to_line, LINE)
    to_y, bias_sum = call(
        lambda *refs: line_kernel(scale, *refs),
        [VMEM],
        (sds((N_Y, ROWS, TILE)), sds((1, f_out), F32)),
    )(from_line)
    column = exchange(to_y, "y").reshape(f_in, TILE)
    to_x = call(join_kernel, [SMEM] + [VMEM] * 4, sds((N_X, f_in + 6 * width, TILE)))(
        zl, column, stay, f_low, f_high
    )
    block = exchange(to_x, "x")
    other = swap(block)
    whole = sds((width, n_rows), F32)
    room = [
        pltpu.VMEM((f_in, f_out), F32),
        dma((N_X,)),
        pltpu.VMEM((N_LINE, width, TILE), F32),
        dma((N_LINE,)),
    ]
    partly = call(
        own_kernel, [SMEM, VMEM], (weight, weight, whole), room, out_specs=(ANY,) * 3
    )(core, block)
    grad_self, grad_neigh, gf = call(
        other_kernel,
        [SMEM, VMEM] + [ANY] * 3,
        (weight, weight, whole),
        room,
        out_specs=(ANY,) * 3,
        input_output_aliases={2: 0, 3: 1, 4: 2},
    )(core, other, *partly)
    return act, grad_self, grad_neigh, bias_sum.reshape(f_out), gf.T


def solution(mesh):
    grid = Mesh(mesh.devices.reshape(SIZES), AXES)
    in_specs = (P(GRAPH, FEAT), P(GRAPH, None), P(), P(), P(), P(GRAPH + FEAT, None))
    out_specs = (P(GRAPH + FEAT, None), P(), P(), P(), P(GRAPH, FEAT))
    return jax.shard_map(local, mesh=grid, in_specs=in_specs, out_specs=out_specs, check_vma=False)
```

```python
import jax
import jax.numpy as jnp
from jax import lax
from jax.experimental import pallas as pl
from jax.experimental.pallas import tpu as pltpu
from jax.sharding import Mesh, PartitionSpec as P

TILE = 128
BF16 = jnp.bfloat16
F32 = jnp.float32
AXES = ("y", "zh", "x", "zl", "c")
SIZES = (8, 4, 4, 3, 2)
GRAPH = ("y", "zh")
FEAT = ("x", "zl", "c")
LINE = ("zh", "zl")
N_X = 4
N_Y = 8
N_LINE = 12
N_FEAT = 24
ROWS = 72
TAIL = 8
SMEM = pl.BlockSpec(memory_space=pltpu.SMEM)
ANY = pl.BlockSpec(memory_space=pl.ANY)
VMEM = pl.BlockSpec(memory_space=pltpu.VMEM)
PARAMS = pltpu.CompilerParams(vmem_limit_bytes=32 * 1024 * 1024)


def dot(a, b, da, db):
    return lax.dot_general(a, b, (((da,), (db,)), ((), ())), preferred_element_type=F32)


def call(kernel, specs, outs, scratch=(), **kw):
    return pl.pallas_call(
        kernel,
        out_shape=outs,
        in_specs=list(specs),
        out_specs=kw.pop("out_specs", jax.tree.map(lambda _: VMEM, outs)),
        scratch_shapes=list(scratch),
        compiler_params=PARAMS,
        **kw,
    )


def sds(shape, dtype=BF16):
    return jax.ShapeDtypeStruct(shape, dtype)


def lanes(b):
    return slice(b * TILE, (b + 1) * TILE)


def band(parts, adj):
    return dot(jnp.concatenate(parts, axis=1), adj, 1, 1)


def prepare_kernel(feats, out, held, sem):
    copy = pltpu.make_async_copy(feats, held, sem)
    copy.start()
    copy.wait()
    for t in range(N_FEAT):
        out[t] = held[:, lanes(t)]


def load_kernel(tile, adjacency, *refs):
    rows = pl.ds(pl.multiple_of(tile[0] * TILE, TILE), TILE)
    sources, targets, sems = (adjacency.at[rows],) + refs[:4], refs[4:-1], refs[-1]
    copies = [
        pltpu.make_async_copy(s, d, sems.at[i])
        for i, (s, d) in enumerate(zip(sources, targets, strict=True))
    ]
    for c in copies:
        c.start()
    for c in copies:
        c.wait()


def sides(core, f, n):
    first = core[0] == 0
    return jnp.where(first, f, n), jnp.where(first, n, f)


def forward_kernel(
    core, near, far, own, adj, ws, wn, bias, cot, act, grad, keep, send, back, scaled
):
    a = adj[...]
    degree = (1.0 + dot(jnp.ones((8, 3 * TILE), BF16), a, 1, 1))[:1]
    low, high = sides(core, far[...], near[...])
    m = (band((low, own[...], high), a) / degree).astype(BF16)
    x = own[...]
    pre = dot(x, ws[...], 0, 0) + dot(m, wn[...], 0, 0) + bias[...]
    s = 1.0 / (1.0 + jnp.exp(-pre))
    act[...] = (pre * s).astype(BF16)
    g = (cot[...].astype(F32) * s * (1.0 + pre * (1.0 - s))).astype(BF16)
    grad[...] = g
    first = core[0] == 0
    keep[...] = jnp.where(first, x, m)
    send[:576] = jnp.where(first, m, x)
    for b in range(4):
        send[576 + b * TILE : 576 + (b + 1) * TILE] = g[:, lanes(b)]
    back[...] = dot(ws[...], g, 1, 1).astype(BF16)
    rounded = dot(wn[...], g, 1, 1).astype(BF16).astype(F32)
    scale = (rounded / degree).astype(BF16)
    scaled[...] = scale
    send[576 + 4 * TILE :] = scale


def partial_kernel(keep, grad, recv, out):
    f_in = keep.shape[0]
    rows = [recv[f_in + b * TILE : f_in + (b + 1) * TILE] for b in range(N_X)]
    g = jnp.concatenate([grad[...], jnp.concatenate(rows, axis=1)], axis=0)
    total = dot(jnp.concatenate([keep[...], recv[:f_in]], axis=1), g, 1, 0)
    sums = jnp.sum(g.astype(F32), axis=0, keepdims=True)
    parts = [sums[:, lanes(b)] for b in range(N_X)]
    tail = jnp.concatenate(parts + [jnp.zeros((TAIL - N_X, TILE), F32)], axis=0)
    for b in range(N_X):
        out[b] = jnp.concatenate([total[:, lanes(b)], tail], axis=0).astype(BF16)


def summed(recv):
    total = recv[0].astype(F32)
    for d in range(1, recv.shape[0]):
        total += recv[d].astype(F32)
    return total


def x_kernel(recv, act, out, act_out):
    act_out[...] = act[...]
    total = summed(recv)
    tail = total[N_Y * ROWS :]
    for d in range(N_Y):
        out[d] = jnp.concatenate([total[d * ROWS : (d + 1) * ROWS], tail], axis=0).astype(BF16)


def y_kernel(recv, out):
    rounded = summed(recv).astype(BF16)
    for d in range(N_LINE):
        out[d] = rounded


def line_kernel(scale, recv, out, bias):
    total = summed(recv) * scale
    bias[...] = jnp.concatenate([total[ROWS + b : ROWS + b + 1] for b in range(N_X)], axis=1)
    rounded = total[:ROWS].astype(BF16)
    for d in range(N_Y):
        out[d] = rounded


def feat_kernel(core, zl, recv, far, own, adj, back, stay, up, down, parts):
    low, high = sides(core, far[...], recv[recv.shape[0] - own.shape[0] :])
    total = back[...].astype(F32) + band((low, own[...], high), adj[...])
    width = parts.shape[1]
    for i in range(N_FEAT):
        parts[i] = total[i * width : (i + 1) * width]
    for shift, out in enumerate((stay, up, down)):
        at = 2 * lax.rem(zl[0] + shift, 3)
        for d in range(N_X):
            pair = jnp.concatenate([parts[6 * d + at], parts[6 * d + at + 1]], axis=0)
            out[d] = pair.astype(BF16)


def join_kernel(zl, grads, stay, low, high, out):
    f_in = grads.shape[0]
    pair = stay.shape[1]
    whole = grads[...]
    place = zl[0]
    for d in range(N_X):
        out[d, :f_in] = whole
        for p in range(3):
            far = jnp.where(place == (p + 1) % 3, low[d], high[d])
            out[d, f_in + p * pair : f_in + (p + 1) * pair] = jnp.where(place == p, stay[d], far)


def halves(block, held, copies):
    for d in range(N_X):
        held[:, lanes(d)] = block[d, : held.shape[0]].astype(F32)
        copies(d)


def send_half(held, sems, first, yes, no):
    def copies(d):
        @pl.when(first)
        def _():
            pltpu.make_async_copy(held.at[:, lanes(d)], yes.at[:, lanes(d)], sems.at[d]).start()

        @pl.when(jnp.logical_not(first))
        def _():
            pltpu.make_async_copy(held.at[:, lanes(d)], no.at[:, lanes(d)], sems.at[d]).start()

    return copies


def finish(held, sems, out):
    for d in range(N_X):
        pltpu.make_async_copy(held.at[:, lanes(d)], out.at[:, lanes(d)], sems.at[d]).wait()


def columns(core, source, block, gf, part, sems):
    width = part.shape[1]
    f_in = block.shape[1] - 6 * width
    first = core == 0
    copies = []
    for d in range(N_X):
        rows = block[d, f_in:].astype(F32)
        for p in range(3):
            k = 3 * d + p
            even = rows[2 * p * width : (2 * p + 1) * width]
            odd = rows[(2 * p + 1) * width : (2 * p + 2) * width]
            at = pl.ds(pl.multiple_of((2 * k + source) * TILE, TILE), TILE)
            part[k] = jnp.where(first, even, odd)
            copies.append(pltpu.make_async_copy(part.at[k], gf.at[:, at], sems.at[k]))
            copies[-1].start()
    return copies


def own_kernel(core, block, gs, gn, gf, held, sems, part, part_sems):
    halves(block, held, send_half(held, sems, core[0] == 0, gs, gn))
    copies = columns(core[0], core[0], block, gf, part, part_sems)
    finish(held, sems, gs)
    for c in copies:
        c.wait()


def other_kernel(core, block, gs_in, gn_in, gf_in, gs, gn, gf, held, sems, part, part_sems):
    halves(block, held, send_half(held, sems, core[0] == 0, gn, gs))
    copies = columns(core[0], 1 - core[0], block, gf, part, part_sems)
    finish(held, sems, gs)
    for c in copies:
        c.wait()


def exchange(x, axis):
    return lax.all_to_all(x, axis, split_axis=0, concat_axis=0, tiled=False)


def across(x):
    pairs = [(2 * k + 1, 2 * k + 2) for k in range(383)]
    pairs += [(b, a) for a, b in pairs]
    return lax.ppermute(x, AXES, pairs)

def swap(x):
    return lax.ppermute(x, "c", [(0, 1), (1, 0)])


def local(features, adjacency, w_self, w_neigh, bias_out, cotangent):
    n_rows, width = features.shape
    f_in, f_out = w_self.shape
    scale = (n_rows * 32) ** -0.5
    core = lax.axis_index("c").astype(jnp.int32).reshape(1)
    tile = lax.axis_index(FEAT).astype(jnp.int32).reshape(1)
    dma = pltpu.SemaphoreType.DMA
    wide = sds((f_in, TILE))
    weight = sds((f_in, f_out), F32)

    def pinned(x):
        return pltpu.with_memory_space_constraint(x, pltpu.HBM)

    pieces = call(
        prepare_kernel, [ANY], sds((N_FEAT, width, TILE)), [pltpu.VMEM((width, n_rows), BF16), dma]
    )(pinned(features.T))
    own = exchange(pieces, FEAT).reshape(f_in, TILE)
    near, far = swap(own), across(own)
    held = call(
        load_kernel,
        [SMEM] + [ANY] * 5,
        (
            sds((TILE, 3 * TILE)),
            sds((f_in, f_out)),
            sds((f_in, f_out)),
            sds((1, f_out), F32),
            sds((TILE, f_out)),
        ),
        [dma((5,))],
    )(tile, *map(pinned, (adjacency, w_self, w_neigh, bias_out.reshape(1, f_out), cotangent)))
    near, far, held = lax.optimization_barrier((near, far, held))
    adj = held[0]
    act, grad, keep, send, back, scaled = call(
        forward_kernel,
        [SMEM] + [VMEM] * 8,
        (sds((TILE, f_out)), sds((TILE, f_out)), wide, sds((2 * f_in + f_out, TILE)), wide, wide),
    )(core, near, far, own, *held)
    recv = swap(send)
    s_far = across(scaled)
    partial = call(partial_kernel, [VMEM] * 3, sds((N_X, f_in + TAIL, TILE)))(keep, grad, recv)
    from_x = exchange(partial, "x")
    to_y, act = call(
        x_kernel, [VMEM] * 2, (sds((N_Y, ROWS + TAIL, TILE)), sds((TILE, f_out)))
    )(from_x, act)
    from_y = exchange(to_y, "y")
    from_y, s_far = lax.optimization_barrier((from_y, s_far))
    from_line = exchange(call(y_kernel, [VMEM], sds((N_LINE, ROWS + TAIL, TILE)))(from_y), LINE)
    zl = lax.axis_index("zl").astype(jnp.int32).reshape(1)
    pair = sds((N_X, 2 * width, TILE))
    stay, up, down = call(
        feat_kernel,
        [SMEM] * 2 + [VMEM] * 5,
        (pair,) * 3,
        [pltpu.VMEM((N_FEAT, width, TILE), F32)],
    )(core, zl, recv, s_far, scaled, adj, back)
    f_low = lax.ppermute(up, "zl", [(i, (i + 1) % 3) for i in range(3)])
    f_high = lax.ppermute(down, "zl", [(i, (i + 2) % 3) for i in range(3)])
    from_line, f_low, f_high = lax.optimization_barrier((from_line, f_low, f_high))
    to_y, bias_sum = call(
        lambda *refs: line_kernel(scale, *refs),
        [VMEM],
        (sds((N_Y, ROWS, TILE)), sds((1, f_out), F32)),
    )(from_line)
    column = exchange(to_y, "y").reshape(f_in, TILE)
    to_x = call(join_kernel, [SMEM] + [VMEM] * 4, sds((N_X, f_in + 6 * width, TILE)))(
        zl, column, stay, f_low, f_high
    )
    block = exchange(to_x, "x")
    other = swap(block)
    whole = sds((width, n_rows), F32)
    room = [
        pltpu.VMEM((f_in, f_out), F32),
        dma((N_X,)),
        pltpu.VMEM((N_LINE, width, TILE), F32),
        dma((N_LINE,)),
    ]
    partly = call(
        own_kernel, [SMEM, VMEM], (weight, weight, whole), room, out_specs=(ANY,) * 3
    )(core, block)
    grad_self, grad_neigh, gf = call(
        other_kernel,
        [SMEM, VMEM] + [ANY] * 3,
        (weight, weight, whole),
        room,
        out_specs=(ANY,) * 3,
        input_output_aliases={2: 0, 3: 1, 4: 2},
    )(core, other, *partly)
    return act, grad_self, grad_neigh, bias_sum.reshape(f_out), gf.T


def solution(mesh):
    grid = Mesh(mesh.devices.reshape(SIZES), AXES)
    in_specs = (P(GRAPH, FEAT), P(GRAPH, None), P(), P(), P(), P(GRAPH + FEAT, None))
    out_specs = (P(GRAPH + FEAT, None), P(), P(), P(), P(GRAPH, FEAT))
    return jax.shard_map(local, mesh=grid, in_specs=in_specs, out_specs=out_specs, check_vma=False)
```

```python
import jax
import jax.numpy as jnp
from jax import lax
from jax.experimental import pallas as pl
from jax.experimental.pallas import tpu as pltpu
from jax.sharding import Mesh, PartitionSpec as P

TILE = 128
BF16 = jnp.bfloat16
F32 = jnp.float32
AXES = ("y", "zh", "x", "zl", "c")
SIZES = (8, 4, 4, 3, 2)
GRAPH = ("y", "zh")
FEAT = ("x", "zl", "c")
LINE = ("zh", "zl")
PLANE = ("y", "zl")
N_X = 4
N_Y = 8
N_LINE = 12
N_FEAT = 24
ROWS = 72
THIRD = 24
TAIL = 8
SMEM = pl.BlockSpec(memory_space=pltpu.SMEM)
ANY = pl.BlockSpec(memory_space=pl.ANY)
VMEM = pl.BlockSpec(memory_space=pltpu.VMEM)
PARAMS = pltpu.CompilerParams(vmem_limit_bytes=32 * 1024 * 1024)


def dot(a, b, da, db):
    return lax.dot_general(a, b, (((da,), (db,)), ((), ())), preferred_element_type=F32)


def call(kernel, specs, outs, scratch=(), **kw):
    return pl.pallas_call(
        kernel,
        out_shape=outs,
        in_specs=list(specs),
        out_specs=kw.pop("out_specs", jax.tree.map(lambda _: VMEM, outs)),
        scratch_shapes=list(scratch),
        compiler_params=PARAMS,
        **kw,
    )


def sds(shape, dtype=BF16):
    return jax.ShapeDtypeStruct(shape, dtype)


def lanes(b):
    return slice(b * TILE, (b + 1) * TILE)


def band(parts, adj):
    return dot(jnp.concatenate(parts, axis=1), adj, 1, 1)


def prepare_kernel(feats, out, held, sem):
    copy = pltpu.make_async_copy(feats, held, sem)
    copy.start()
    copy.wait()
    for t in range(N_FEAT):
        out[t] = held[:, lanes(t)]


def load_kernel(tile, adjacency, *refs):
    rows = pl.ds(pl.multiple_of(tile[0] * TILE, TILE), TILE)
    sources, targets, sems = (adjacency.at[rows],) + refs[:4], refs[4:-1], refs[-1]
    copies = [
        pltpu.make_async_copy(s, d, sems.at[i])
        for i, (s, d) in enumerate(zip(sources, targets, strict=True))
    ]
    for c in copies:
        c.start()
    for c in copies:
        c.wait()


def sides(core, f, n):
    first = core[0] == 0
    return jnp.where(first, f, n), jnp.where(first, n, f)


def early_kernel(own, adj, ws, bias, inner, degree, pre):
    a = adj[...]
    degree[...] = 1.0 + dot(jnp.ones((8, 3 * TILE), BF16), a, 1, 1)
    x = own[...]
    inner[...] = dot(x, a[:, lanes(1)], 1, 1)
    pre[...] = dot(x, ws[...], 0, 0) + bias[...]


def forward_kernel(
    core, near, far, own, adj, ws, wn, cot, inner, degree, pre_self,
    act, grad, keep, send, back, scaled,
):
    count = degree[:1]
    edges = jnp.concatenate([adj[:, lanes(0)], adj[:, lanes(2)]], axis=1)
    tiles = jnp.concatenate(sides(core, far[...], near[...]), axis=1)
    m = ((inner[...] + dot(tiles, edges, 1, 1)) / count).astype(BF16)
    pre = pre_self[...] + dot(m, wn[...], 0, 0)
    s = 1.0 / (1.0 + jnp.exp(-pre))
    act[...] = (pre * s).astype(BF16)
    g = (cot[...].astype(F32) * s * (1.0 + pre * (1.0 - s))).astype(BF16)
    grad[...] = g
    x = own[...]
    first = core[0] == 0
    keep[...] = jnp.where(first, x, m)
    send[:576] = jnp.where(first, m, x)
    for b in range(4):
        send[576 + b * TILE : 576 + (b + 1) * TILE] = g[:, lanes(b)]
    back[...] = dot(ws[...], g, 1, 1).astype(BF16)
    rounded = dot(wn[...], g, 1, 1).astype(BF16).astype(F32)
    scale = (rounded / count).astype(BF16)
    scaled[...] = scale
    send[576 + 4 * TILE :] = scale


def partial_kernel(keep, grad, recv, act, out, act_out):
    act_out[...] = act[...]
    f_in = keep.shape[0]
    rows = [recv[f_in + b * TILE : f_in + (b + 1) * TILE] for b in range(N_X)]
    g = jnp.concatenate([grad[...], jnp.concatenate(rows, axis=1)], axis=0)
    total = dot(jnp.concatenate([keep[...], recv[:f_in]], axis=1), g, 1, 0)
    sums = jnp.sum(g.astype(F32), axis=0, keepdims=True)
    parts = [sums[:, lanes(b)] for b in range(N_X)]
    tail = jnp.concatenate(parts + [jnp.zeros((TAIL - N_X, TILE), F32)], axis=0)
    for b in range(N_X):
        out[b] = jnp.concatenate([total[:, lanes(b)], tail], axis=0).astype(BF16)


def summed(recv):
    total = recv[0].astype(F32)
    for d in range(1, recv.shape[0]):
        total += recv[d].astype(F32)
    return total


def x_kernel(recv, out):
    total = summed(recv)
    tail = total[N_Y * ROWS :]
    for d in range(N_Y):
        out[d] = jnp.concatenate([total[d * ROWS : (d + 1) * ROWS], tail], axis=0).astype(BF16)


def y_kernel(recv, out):
    total = summed(recv)
    tail = total[ROWS:]
    for zl in range(3):
        rounded = jnp.concatenate([total[zl * THIRD : (zl + 1) * THIRD], tail], axis=0).astype(BF16)
        for zh in range(4):
            out[3 * zh + zl] = rounded


def line_kernel(scale, recv, out, bias):
    total = summed(recv) * scale
    bias[...] = jnp.concatenate([total[THIRD + b : THIRD + b + 1] for b in range(N_X)], axis=1)
    rounded = total[:THIRD].astype(BF16)
    for d in range(3 * N_Y):
        out[d] = rounded


def feat_kernel(core, zl, recv, far, own, adj, back, stay, up, down, parts):
    low, high = sides(core, far[...], recv[recv.shape[0] - own.shape[0] :])
    total = back[...].astype(F32) + band((low, own[...], high), adj[...])
    width = parts.shape[1]
    for i in range(N_FEAT):
        parts[i] = total[i * width : (i + 1) * width]
    for shift, out in enumerate((stay, up, down)):
        at = 2 * lax.rem(zl[0] + shift, 3)
        for d in range(N_X):
            pair = jnp.concatenate([parts[6 * d + at], parts[6 * d + at + 1]], axis=0)
            out[d] = pair.astype(BF16)


def join_kernel(zl, grads, stay, low, high, out):
    f_in = grads.shape[0]
    pair = stay.shape[1]
    whole = grads[...]
    place = zl[0]
    for d in range(N_X):
        out[d, :f_in] = whole
        for p in range(3):
            far = jnp.where(place == (p + 1) % 3, low[d], high[d])
            out[d, f_in + p * pair : f_in + (p + 1) * pair] = jnp.where(place == p, stay[d], far)


def halves(block, held, copies):
    for d in range(N_X):
        held[:, lanes(d)] = block[d, : held.shape[0]].astype(F32)
        copies(d)


def send_half(held, sems, first, yes, no):
    def copies(d):
        @pl.when(first)
        def _():
            pltpu.make_async_copy(held.at[:, lanes(d)], yes.at[:, lanes(d)], sems.at[d]).start()

        @pl.when(jnp.logical_not(first))
        def _():
            pltpu.make_async_copy(held.at[:, lanes(d)], no.at[:, lanes(d)], sems.at[d]).start()

    return copies


def finish(held, sems, out):
    for d in range(N_X):
        pltpu.make_async_copy(held.at[:, lanes(d)], out.at[:, lanes(d)], sems.at[d]).wait()


def columns(core, source, block, gf, part, sems):
    width = part.shape[1]
    f_in = block.shape[1] - 6 * width
    first = core == 0
    copies = []
    for d in range(N_X):
        rows = block[d, f_in:].astype(F32)
        for p in range(3):
            k = 3 * d + p
            even = rows[2 * p * width : (2 * p + 1) * width]
            odd = rows[(2 * p + 1) * width : (2 * p + 2) * width]
            at = pl.ds(pl.multiple_of((2 * k + source) * TILE, TILE), TILE)
            part[k] = jnp.where(first, even, odd)
            copies.append(pltpu.make_async_copy(part.at[k], gf.at[:, at], sems.at[k]))
            copies[-1].start()
    return copies


def own_kernel(core, block, gs, gn, gf, held, sems, part, part_sems):
    halves(block, held, send_half(held, sems, core[0] == 0, gs, gn))
    copies = columns(core[0], core[0], block, gf, part, part_sems)
    finish(held, sems, gs)
    for c in copies:
        c.wait()


def other_kernel(core, block, gs_in, gn_in, gf_in, gs, gn, gf, held, sems, part, part_sems):
    halves(block, held, send_half(held, sems, core[0] == 0, gn, gs))
    copies = columns(core[0], 1 - core[0], block, gf, part, part_sems)
    finish(held, sems, gs)
    for c in copies:
        c.wait()


def exchange(x, axis):
    return lax.all_to_all(x, axis, split_axis=0, concat_axis=0, tiled=False)


def across(x):
    pairs = [(2 * k + 1, 2 * k + 2) for k in range(383)]
    pairs += [(b, a) for a, b in pairs]
    return lax.ppermute(x, AXES, pairs)

def swap(x):
    return lax.ppermute(x, "c", [(0, 1), (1, 0)])


def local(features, adjacency, w_self, w_neigh, bias_out, cotangent):
    n_rows, width = features.shape
    f_in, f_out = w_self.shape
    scale = (n_rows * 32) ** -0.5
    core = lax.axis_index("c").astype(jnp.int32).reshape(1)
    tile = lax.axis_index(FEAT).astype(jnp.int32).reshape(1)
    dma = pltpu.SemaphoreType.DMA
    wide = sds((f_in, TILE))
    weight = sds((f_in, f_out), F32)

    def pinned(x):
        return pltpu.with_memory_space_constraint(x, pltpu.HBM)

    pieces = call(
        prepare_kernel, [ANY], sds((N_FEAT, width, TILE)), [pltpu.VMEM((width, n_rows), BF16), dma]
    )(pinned(features.T))
    own = exchange(pieces, FEAT).reshape(f_in, TILE)
    near, far = swap(own), across(own)
    held = call(
        load_kernel,
        [SMEM] + [ANY] * 5,
        (
            sds((TILE, 3 * TILE)),
            sds((f_in, f_out)),
            sds((f_in, f_out)),
            sds((1, f_out), F32),
            sds((TILE, f_out)),
        ),
        [dma((5,))],
    )(tile, *map(pinned, (adjacency, w_self, w_neigh, bias_out.reshape(1, f_out), cotangent)))
    adj, ws, wn, bias, cot = held
    early = call(
        early_kernel,
        [VMEM] * 4,
        (sds((f_in, TILE), F32), sds((8, TILE), F32), sds((TILE, f_out), F32)),
    )(own, adj, ws, bias)
    near, far, early = lax.optimization_barrier((near, far, early))
    act, grad, keep, send, back, scaled = call(
        forward_kernel,
        [SMEM] + [VMEM] * 10,
        (sds((TILE, f_out)), sds((TILE, f_out)), wide, sds((2 * f_in + f_out, TILE)), wide, wide),
    )(core, near, far, own, adj, ws, wn, cot, *early)
    recv = swap(send)
    s_far = across(scaled)
    partial, act = call(
        partial_kernel, [VMEM] * 4, (sds((N_X, f_in + TAIL, TILE)), sds((TILE, f_out)))
    )(keep, grad, recv, act)
    from_x = exchange(partial, "x")
    from_x, s_far = lax.optimization_barrier((from_x, s_far))
    zl = lax.axis_index("zl").astype(jnp.int32).reshape(1)
    pair = sds((N_X, 2 * width, TILE))
    stay, up, down = call(
        feat_kernel,
        [SMEM] * 2 + [VMEM] * 5,
        (pair,) * 3,
        [pltpu.VMEM((N_FEAT, width, TILE), F32)],
    )(core, zl, recv, s_far, scaled, adj, back)
    from_x, stay, up, down = lax.optimization_barrier((from_x, stay, up, down))
    from_y = exchange(call(x_kernel, [VMEM], sds((N_Y, ROWS + TAIL, TILE)))(from_x), "y")
    from_line = exchange(call(y_kernel, [VMEM], sds((N_LINE, THIRD + TAIL, TILE)))(from_y), LINE)
    f_low = lax.ppermute(up, "zl", [(i, (i + 1) % 3) for i in range(3)])
    f_high = lax.ppermute(down, "zl", [(i, (i + 2) % 3) for i in range(3)])
    to_plane, bias_sum = call(
        lambda *refs: line_kernel(scale, *refs),
        [VMEM],
        (sds((3 * N_Y, THIRD, TILE)), sds((1, f_out), F32)),
    )(from_line)
    column = exchange(to_plane, PLANE).reshape(f_in, TILE)
    to_x = call(join_kernel, [SMEM] + [VMEM] * 4, sds((N_X, f_in + 6 * width, TILE)))(
        zl, column, stay, f_low, f_high
    )
    block = exchange(to_x, "x")
    other = swap(block)
    whole = sds((width, n_rows), F32)
    room = [
        pltpu.VMEM((f_in, f_out), F32),
        dma((N_X,)),
        pltpu.VMEM((N_LINE, width, TILE), F32),
        dma((N_LINE,)),
    ]
    partly = call(
        own_kernel, [SMEM, VMEM], (weight, weight, whole), room, out_specs=(ANY,) * 3
    )(core, block)
    grad_self, grad_neigh, gf = call(
        other_kernel,
        [SMEM, VMEM] + [ANY] * 3,
        (weight, weight, whole),
        room,
        out_specs=(ANY,) * 3,
        input_output_aliases={2: 0, 3: 1, 4: 2},
    )(core, other, *partly)
    return act, grad_self, grad_neigh, bias_sum.reshape(f_out), gf.T


def solution(mesh):
    grid = Mesh(mesh.devices.reshape(SIZES), AXES)
    in_specs = (P(GRAPH, FEAT), P(GRAPH, None), P(), P(), P(), P(GRAPH + FEAT, None))
    out_specs = (P(GRAPH + FEAT, None), P(), P(), P(), P(GRAPH, FEAT))
    return jax.shard_map(local, mesh=grid, in_specs=in_specs, out_specs=out_specs, check_vma=False)
```

```python
import jax
import jax.numpy as jnp
from jax import lax
from jax.experimental import pallas as pl
from jax.experimental.pallas import tpu as pltpu
from jax.sharding import Mesh, PartitionSpec as P

TILE = 128
BF16 = jnp.bfloat16
F32 = jnp.float32
AXES = ("y", "zh", "x", "zl", "c")
SIZES = (8, 4, 4, 3, 2)
GRAPH = ("y", "zh")
FEAT = ("x", "zl", "c")
LINE = ("zh", "zl")
BLOCK = ("x", "zl")
N_X = 4
N_Y = 8
N_LINE = 12
N_FEAT = 24
ROWS = 72
THIRD = 24
TAIL = 8
SMEM = pl.BlockSpec(memory_space=pltpu.SMEM)
ANY = pl.BlockSpec(memory_space=pl.ANY)
VMEM = pl.BlockSpec(memory_space=pltpu.VMEM)
PARAMS = pltpu.CompilerParams(vmem_limit_bytes=32 * 1024 * 1024)


def dot(a, b, da, db):
    return lax.dot_general(a, b, (((da,), (db,)), ((), ())), preferred_element_type=F32)


def call(kernel, specs, outs, scratch=(), **kw):
    return pl.pallas_call(
        kernel,
        out_shape=outs,
        in_specs=list(specs),
        out_specs=kw.pop("out_specs", jax.tree.map(lambda _: VMEM, outs)),
        scratch_shapes=list(scratch),
        compiler_params=PARAMS,
        **kw,
    )


def sds(shape, dtype=BF16):
    return jax.ShapeDtypeStruct(shape, dtype)


def lanes(b):
    return slice(b * TILE, (b + 1) * TILE)


def band(parts, adj):
    return dot(jnp.concatenate(parts, axis=1), adj, 1, 1)


def prepare_kernel(feats, out, held, sem):
    copy = pltpu.make_async_copy(feats, held, sem)
    copy.start()
    copy.wait()
    for t in range(N_FEAT):
        out[t] = held[:, lanes(t)]


def load_kernel(tile, adjacency, *refs):
    rows = pl.ds(pl.multiple_of(tile[0] * TILE, TILE), TILE)
    sources, targets, sems = (adjacency.at[rows],) + refs[:4], refs[4:-1], refs[-1]
    copies = [
        pltpu.make_async_copy(s, d, sems.at[i])
        for i, (s, d) in enumerate(zip(sources, targets, strict=True))
    ]
    for c in copies:
        c.start()
    for c in copies:
        c.wait()


def sides(core, f, n):
    first = core[0] == 0
    return jnp.where(first, f, n), jnp.where(first, n, f)


def early_kernel(own, adj, ws, bias, inner, degree, pre):
    a = adj[...]
    degree[...] = 1.0 + dot(jnp.ones((8, 3 * TILE), BF16), a, 1, 1)
    x = own[...]
    inner[...] = dot(x, a[:, lanes(1)], 1, 1)
    pre[...] = dot(x, ws[...], 0, 0) + bias[...]


def forward_kernel(
    core, near, far, own, adj, ws, wn, cot, inner, degree, pre_self,
    act, grad, keep, send, back, scaled,
):
    count = degree[:1]
    edges = jnp.concatenate([adj[:, lanes(0)], adj[:, lanes(2)]], axis=1)
    tiles = jnp.concatenate(sides(core, far[...], near[...]), axis=1)
    m = ((inner[...] + dot(tiles, edges, 1, 1)) / count).astype(BF16)
    pre = pre_self[...] + dot(m, wn[...], 0, 0)
    s = 1.0 / (1.0 + jnp.exp(-pre))
    act[...] = (pre * s).astype(BF16)
    g = (cot[...].astype(F32) * s * (1.0 + pre * (1.0 - s))).astype(BF16)
    grad[...] = g
    x = own[...]
    first = core[0] == 0
    keep[...] = jnp.where(first, x, m)
    send[:576] = jnp.where(first, m, x)
    for b in range(4):
        send[576 + b * TILE : 576 + (b + 1) * TILE] = g[:, lanes(b)]
    back[...] = dot(ws[...], g, 1, 1).astype(BF16)
    rounded = dot(wn[...], g, 1, 1).astype(BF16).astype(F32)
    scale = (rounded / count).astype(BF16)
    scaled[...] = scale
    send[576 + 4 * TILE :] = scale


def partial_kernel(keep, grad, recv, act, out, act_out):
    act_out[...] = act[...]
    f_in = keep.shape[0]
    rows = [recv[f_in + b * TILE : f_in + (b + 1) * TILE] for b in range(N_X)]
    g = jnp.concatenate([grad[...], jnp.concatenate(rows, axis=1)], axis=0)
    total = dot(jnp.concatenate([keep[...], recv[:f_in]], axis=1), g, 1, 0)
    sums = jnp.sum(g.astype(F32), axis=0, keepdims=True)
    parts = [sums[:, lanes(b)] for b in range(N_X)]
    tail = jnp.concatenate(parts + [jnp.zeros((TAIL - N_X, TILE), F32)], axis=0)
    for b in range(N_X):
        out[b] = jnp.concatenate([total[:, lanes(b)], tail], axis=0).astype(BF16)


def summed(recv):
    total = recv[0].astype(F32)
    for d in range(1, recv.shape[0]):
        total += recv[d].astype(F32)
    return total


def x_kernel(recv, out):
    total = summed(recv)
    tail = total[N_Y * ROWS :]
    for d in range(N_Y):
        out[d] = jnp.concatenate([total[d * ROWS : (d + 1) * ROWS], tail], axis=0).astype(BF16)


def y_kernel(recv, out):
    total = summed(recv)
    tail = total[ROWS:]
    for zl in range(3):
        rounded = jnp.concatenate([total[zl * THIRD : (zl + 1) * THIRD], tail], axis=0).astype(BF16)
        for zh in range(4):
            out[3 * zh + zl] = rounded


def line_kernel(scale, recv, out, bias):
    total = summed(recv) * scale
    bias[...] = jnp.concatenate([total[THIRD + b : THIRD + b + 1] for b in range(N_X)], axis=1)
    rounded = total[:THIRD].astype(BF16)
    for d in range(N_Y):
        out[d] = rounded


def feat_kernel(core, recv, far, own, adj, back, out):
    low, high = sides(core, far[...], recv[recv.shape[0] - own.shape[0] :])
    total = back[...].astype(F32) + band((low, own[...], high), adj[...])
    pair = out.shape[1]
    for d in range(N_LINE):
        out[d] = total[d * pair : (d + 1) * pair].astype(BF16)


def join_kernel(grads, feats, out):
    rows = grads.shape[0]
    whole = grads[...]
    for d in range(N_LINE):
        out[d, :rows] = whole
        out[d, rows:] = feats[d]


def halves(block, held, copies):
    for x in range(N_X):
        for zl in range(3):
            rows = block[3 * x + zl, : N_Y * THIRD].astype(F32)
            for y in range(N_Y):
                at = y * ROWS + zl * THIRD
                held[at : at + THIRD, lanes(x)] = rows[y * THIRD : (y + 1) * THIRD]
        copies(x)


def send_half(held, sems, first, yes, no):
    def copies(d):
        @pl.when(first)
        def _():
            pltpu.make_async_copy(held.at[:, lanes(d)], yes.at[:, lanes(d)], sems.at[d]).start()

        @pl.when(jnp.logical_not(first))
        def _():
            pltpu.make_async_copy(held.at[:, lanes(d)], no.at[:, lanes(d)], sems.at[d]).start()

    return copies


def finish(held, sems, out):
    for d in range(N_X):
        pltpu.make_async_copy(held.at[:, lanes(d)], out.at[:, lanes(d)], sems.at[d]).wait()


def columns(core, source, block, gf, part, sems):
    width = part.shape[1]
    first = core == 0
    copies = []
    for d in range(N_LINE):
        rows = block[d, N_Y * THIRD :].astype(F32)
        at = pl.ds(pl.multiple_of((2 * d + source) * TILE, TILE), TILE)
        part[d] = jnp.where(first, rows[:width], rows[width:])
        copies.append(pltpu.make_async_copy(part.at[d], gf.at[:, at], sems.at[d]))
        copies[-1].start()
    return copies


def own_kernel(core, block, gs, gn, gf, held, sems, part, part_sems):
    halves(block, held, send_half(held, sems, core[0] == 0, gs, gn))
    copies = columns(core[0], core[0], block, gf, part, part_sems)
    finish(held, sems, gs)
    for c in copies:
        c.wait()


def other_kernel(core, block, gs_in, gn_in, gf_in, gs, gn, gf, held, sems, part, part_sems):
    halves(block, held, send_half(held, sems, core[0] == 0, gn, gs))
    copies = columns(core[0], 1 - core[0], block, gf, part, part_sems)
    finish(held, sems, gs)
    for c in copies:
        c.wait()


def exchange(x, axis):
    return lax.all_to_all(x, axis, split_axis=0, concat_axis=0, tiled=False)


def across(x):
    pairs = [(2 * k + 1, 2 * k + 2) for k in range(383)]
    pairs += [(b, a) for a, b in pairs]
    return lax.ppermute(x, AXES, pairs)

def swap(x):
    return lax.ppermute(x, "c", [(0, 1), (1, 0)])


def local(features, adjacency, w_self, w_neigh, bias_out, cotangent):
    n_rows, width = features.shape
    f_in, f_out = w_self.shape
    scale = (n_rows * 32) ** -0.5
    core = lax.axis_index("c").astype(jnp.int32).reshape(1)
    tile = lax.axis_index(FEAT).astype(jnp.int32).reshape(1)
    dma = pltpu.SemaphoreType.DMA
    wide = sds((f_in, TILE))
    weight = sds((f_in, f_out), F32)

    def pinned(x):
        return pltpu.with_memory_space_constraint(x, pltpu.HBM)

    pieces = call(
        prepare_kernel, [ANY], sds((N_FEAT, width, TILE)), [pltpu.VMEM((width, n_rows), BF16), dma]
    )(pinned(features.T))
    own = exchange(pieces, FEAT).reshape(f_in, TILE)
    near, far = swap(own), across(own)
    held = call(
        load_kernel,
        [SMEM] + [ANY] * 5,
        (
            sds((TILE, 3 * TILE)),
            sds((f_in, f_out)),
            sds((f_in, f_out)),
            sds((1, f_out), F32),
            sds((TILE, f_out)),
        ),
        [dma((5,))],
    )(tile, *map(pinned, (adjacency, w_self, w_neigh, bias_out.reshape(1, f_out), cotangent)))
    adj, ws, wn, bias, cot = held
    early = call(
        early_kernel,
        [VMEM] * 4,
        (sds((f_in, TILE), F32), sds((8, TILE), F32), sds((TILE, f_out), F32)),
    )(own, adj, ws, bias)
    near, far, early = lax.optimization_barrier((near, far, early))
    act, grad, keep, send, back, scaled = call(
        forward_kernel,
        [SMEM] + [VMEM] * 10,
        (sds((TILE, f_out)), sds((TILE, f_out)), wide, sds((2 * f_in + f_out, TILE)), wide, wide),
    )(core, near, far, own, adj, ws, wn, cot, *early)
    recv = swap(send)
    s_far = across(scaled)
    partial, act = call(
        partial_kernel, [VMEM] * 4, (sds((N_X, f_in + TAIL, TILE)), sds((TILE, f_out)))
    )(keep, grad, recv, act)
    from_x = exchange(partial, "x")
    from_x, s_far = lax.optimization_barrier((from_x, s_far))
    feats = call(feat_kernel, [SMEM] + [VMEM] * 5, sds((N_LINE, 2 * width, TILE)))(
        core, recv, s_far, scaled, adj, back
    )
    from_x, feats = lax.optimization_barrier((from_x, feats))
    from_y = exchange(call(x_kernel, [VMEM], sds((N_Y, ROWS + TAIL, TILE)))(from_x), "y")
    from_line = exchange(call(y_kernel, [VMEM], sds((N_LINE, THIRD + TAIL, TILE)))(from_y), LINE)
    to_y_again, bias_sum = call(
        lambda *refs: line_kernel(scale, *refs),
        [VMEM],
        (sds((N_Y, THIRD, TILE)), sds((1, f_out), F32)),
    )(from_line)
    column = exchange(to_y_again, "y").reshape(N_Y * THIRD, TILE)
    to_block = call(join_kernel, [VMEM] * 2, sds((N_LINE, N_Y * THIRD + 2 * width, TILE)))(column, feats)
    block = exchange(to_block, BLOCK)
    other = swap(block)
    whole = sds((width, n_rows), F32)
    room = [
        pltpu.VMEM((f_in, f_out), F32),
        dma((N_X,)),
        pltpu.VMEM((N_LINE, width, TILE), F32),
        dma((N_LINE,)),
    ]
    partly = call(
        own_kernel, [SMEM, VMEM], (weight, weight, whole), room, out_specs=(ANY,) * 3
    )(core, block)
    grad_self, grad_neigh, gf = call(
        other_kernel,
        [SMEM, VMEM] + [ANY] * 3,
        (weight, weight, whole),
        room,
        out_specs=(ANY,) * 3,
        input_output_aliases={2: 0, 3: 1, 4: 2},
    )(core, other, *partly)
    return act, grad_self, grad_neigh, bias_sum.reshape(f_out), gf.T


def solution(mesh):
    grid = Mesh(mesh.devices.reshape(SIZES), AXES)
    in_specs = (P(GRAPH, FEAT), P(GRAPH, None), P(), P(), P(), P(GRAPH + FEAT, None))
    out_specs = (P(GRAPH + FEAT, None), P(), P(), P(), P(GRAPH, FEAT))
    return jax.shard_map(local, mesh=grid, in_specs=in_specs, out_specs=out_specs, check_vma=False)
```

```python
import jax
import jax.numpy as jnp
from jax import lax
from jax.experimental import pallas as pl
from jax.experimental.pallas import tpu as pltpu
from jax.sharding import Mesh, PartitionSpec as P

TILE = 128
BF16 = jnp.bfloat16
F32 = jnp.float32
AXES = ("y", "zh", "x", "zl", "c")
SIZES = (8, 4, 4, 3, 2)
GRAPH = ("y", "zh")
FEAT = ("x", "zl", "c")
LINE = ("zh", "zl")
BLOCK = ("x", "zl")
N_X = 4
N_Y = 8
N_LINE = 12
N_FEAT = 24
ROWS = 72
THIRD = 24
TAIL = 8
SMEM = pl.BlockSpec(memory_space=pltpu.SMEM)
ANY = pl.BlockSpec(memory_space=pl.ANY)
VMEM = pl.BlockSpec(memory_space=pltpu.VMEM)
PARAMS = pltpu.CompilerParams(vmem_limit_bytes=32 * 1024 * 1024)


def dot(a, b, da, db):
    return lax.dot_general(a, b, (((da,), (db,)), ((), ())), preferred_element_type=F32)


def call(kernel, specs, outs, scratch=(), **kw):
    return pl.pallas_call(
        kernel,
        out_shape=outs,
        in_specs=list(specs),
        out_specs=kw.pop("out_specs", jax.tree.map(lambda _: VMEM, outs)),
        scratch_shapes=list(scratch),
        compiler_params=PARAMS,
        **kw,
    )


def sds(shape, dtype=BF16):
    return jax.ShapeDtypeStruct(shape, dtype)


def lanes(b):
    return slice(b * TILE, (b + 1) * TILE)


def band(parts, adj):
    return dot(jnp.concatenate(parts, axis=1), adj, 1, 1)


def prepare_kernel(feats, out, held, sem):
    copy = pltpu.make_async_copy(feats, held, sem)
    copy.start()
    copy.wait()
    for t in range(N_FEAT):
        out[t] = held[:, lanes(t)]


def load_kernel(tile, adjacency, *refs):
    rows = pl.ds(pl.multiple_of(tile[0] * TILE, TILE), TILE)
    sources, targets, sems = (adjacency.at[rows],) + refs[:4], refs[4:-1], refs[-1]
    copies = [
        pltpu.make_async_copy(s, d, sems.at[i])
        for i, (s, d) in enumerate(zip(sources, targets, strict=True))
    ]
    for c in copies:
        c.start()
    for c in copies:
        c.wait()


def sides(core, f, n):
    first = core[0] == 0
    return jnp.where(first, f, n), jnp.where(first, n, f)


def early_kernel(own, adj, ws, bias, inner, degree, pre):
    a = adj[...]
    degree[...] = 1.0 + dot(jnp.ones((8, 3 * TILE), BF16), a, 1, 1)
    x = own[...]
    inner[...] = dot(x, a[:, lanes(1)], 1, 1)
    pre[...] = dot(x, ws[...], 0, 0) + bias[...]


def forward_kernel(
    core, near, far, own, adj, ws, wn, cot, inner, degree, pre_self,
    act, grad, keep, send, back, scaled,
):
    count = degree[:1]
    edges = jnp.concatenate([adj[:, lanes(0)], adj[:, lanes(2)]], axis=1)
    tiles = jnp.concatenate(sides(core, far[...], near[...]), axis=1)
    m = ((inner[...] + dot(tiles, edges, 1, 1)) / count).astype(BF16)
    pre = pre_self[...] + dot(m, wn[...], 0, 0)
    s = 1.0 / (1.0 + jnp.exp(-pre))
    act[...] = (pre * s).astype(BF16)
    g = (cot[...].astype(F32) * s * (1.0 + pre * (1.0 - s))).astype(BF16)
    grad[...] = g
    x = own[...]
    first = core[0] == 0
    keep[...] = jnp.where(first, x, m)
    send[:576] = jnp.where(first, m, x)
    for b in range(4):
        send[576 + b * TILE : 576 + (b + 1) * TILE] = g[:, lanes(b)]
    back[...] = dot(ws[...], g, 1, 1).astype(BF16)
    rounded = dot(wn[...], g, 1, 1).astype(BF16).astype(F32)
    scale = (rounded / count).astype(BF16)
    scaled[...] = scale
    send[576 + 4 * TILE :] = scale


def partial_kernel(keep, grad, recv, act, out, act_out):
    act_out[...] = act[...]
    f_in = keep.shape[0]
    rows = [recv[f_in + b * TILE : f_in + (b + 1) * TILE] for b in range(N_X)]
    g = jnp.concatenate([grad[...], jnp.concatenate(rows, axis=1)], axis=0)
    total = dot(jnp.concatenate([keep[...], recv[:f_in]], axis=1), g, 1, 0)
    sums = jnp.sum(g.astype(F32), axis=0, keepdims=True)
    parts = [sums[:, lanes(b)] for b in range(N_X)]
    tail = jnp.concatenate(parts + [jnp.zeros((TAIL - N_X, TILE), F32)], axis=0)
    for b in range(N_X):
        out[b] = jnp.concatenate([total[:, lanes(b)], tail], axis=0).astype(BF16)


def summed(recv):
    total = recv[0].astype(F32)
    for d in range(1, recv.shape[0]):
        total += recv[d].astype(F32)
    return total


def x_kernel(recv, out):
    total = summed(recv)
    tail = total[N_Y * ROWS :]
    for d in range(N_Y):
        out[d] = jnp.concatenate([total[d * ROWS : (d + 1) * ROWS], tail], axis=0).astype(BF16)


def y_kernel(recv, out):
    total = summed(recv)
    tail = total[ROWS:]
    for zl in range(3):
        rounded = jnp.concatenate([total[zl * THIRD : (zl + 1) * THIRD], tail], axis=0).astype(BF16)
        for zh in range(4):
            out[3 * zh + zl] = rounded


def line_kernel(scale, recv, out, bias):
    total = summed(recv) * scale
    bias[...] = jnp.concatenate([total[THIRD + b : THIRD + b + 1] for b in range(N_X)], axis=1)
    rounded = total[:THIRD].astype(BF16)
    for d in range(N_Y):
        out[d] = rounded


def feat_kernel(core, recv, far, own, adj, back, out):
    low, high = sides(core, far[...], recv[recv.shape[0] - own.shape[0] :])
    total = back[...].astype(F32) + band((low, own[...], high), adj[...])
    pair = out.shape[1]
    for d in range(N_LINE):
        out[d] = total[d * pair : (d + 1) * pair].astype(BF16)


def join_kernel(grads, feats, out):
    rows = grads.shape[0]
    whole = grads[...]
    for d in range(N_LINE):
        out[d, :rows] = whole
        out[d, rows:] = feats[d]


def halves(block, held, copies):
    for x in range(N_X):
        for zl in range(3):
            rows = block[3 * x + zl, : N_Y * THIRD].astype(F32)
            for y in range(N_Y):
                at = y * ROWS + zl * THIRD
                held[at : at + THIRD, lanes(x)] = rows[y * THIRD : (y + 1) * THIRD]
        copies(x)


def send_half(held, sems, first, yes, no):
    def copies(d):
        @pl.when(first)
        def _():
            pltpu.make_async_copy(held.at[:, lanes(d)], yes.at[:, lanes(d)], sems.at[d]).start()

        @pl.when(jnp.logical_not(first))
        def _():
            pltpu.make_async_copy(held.at[:, lanes(d)], no.at[:, lanes(d)], sems.at[d]).start()

    return copies


def finish(held, sems, out):
    for d in range(N_X):
        pltpu.make_async_copy(held.at[:, lanes(d)], out.at[:, lanes(d)], sems.at[d]).wait()


def columns(core, source, block, gf, part, sems):
    width = part.shape[1]
    first = core == 0
    copies = []
    for d in range(N_LINE):
        rows = block[d, N_Y * THIRD :].astype(F32)
        at = pl.ds(pl.multiple_of((2 * d + source) * TILE, TILE), TILE)
        part[d] = jnp.where(first, rows[:width], rows[width:])
        copies.append(pltpu.make_async_copy(part.at[d], gf.at[:, at], sems.at[d]))
        copies[-1].start()
    return copies


def own_kernel(core, block, gs, gn, gf, held, sems, part, part_sems):
    halves(block, held, send_half(held, sems, core[0] == 0, gs, gn))
    copies = columns(core[0], core[0], block, gf, part, part_sems)
    finish(held, sems, gs)
    for c in copies:
        c.wait()


def other_kernel(core, block, gs_in, gn_in, gf_in, gs, gn, gf, held, sems, part, part_sems):
    halves(block, held, send_half(held, sems, core[0] == 0, gn, gs))
    copies = columns(core[0], 1 - core[0], block, gf, part, part_sems)
    finish(held, sems, gs)
    for c in copies:
        c.wait()


def exchange(x, axis):
    return lax.all_to_all(x, axis, split_axis=0, concat_axis=0, tiled=False)


def across(x):
    pairs = [(2 * k + 1, 2 * k + 2) for k in range(383)]
    pairs += [(b, a) for a, b in pairs]
    return lax.ppermute(x, AXES, pairs)

def swap(x):
    return lax.ppermute(x, "c", [(0, 1), (1, 0)])


def local(features, adjacency, w_self, w_neigh, bias_out, cotangent):
    n_rows, width = features.shape
    f_in, f_out = w_self.shape
    scale = (n_rows * 32) ** -0.5
    core = lax.axis_index("c").astype(jnp.int32).reshape(1)
    tile = lax.axis_index(FEAT).astype(jnp.int32).reshape(1)
    dma = pltpu.SemaphoreType.DMA
    wide = sds((f_in, TILE))
    weight = sds((f_in, f_out), F32)

    def pinned(x):
        return pltpu.with_memory_space_constraint(x, pltpu.HBM)

    pieces = call(
        prepare_kernel, [ANY], sds((N_FEAT, width, TILE)), [pltpu.VMEM((width, n_rows), BF16), dma]
    )(pinned(features.T))
    own = exchange(pieces, FEAT).reshape(f_in, TILE)
    near, far = swap(own), across(own)
    held = call(
        load_kernel,
        [SMEM] + [ANY] * 5,
        (
            sds((TILE, 3 * TILE)),
            sds((f_in, f_out)),
            sds((f_in, f_out)),
            sds((1, f_out), F32),
            sds((TILE, f_out)),
        ),
        [dma((5,))],
    )(tile, *map(pinned, (adjacency, w_self, w_neigh, bias_out.reshape(1, f_out), cotangent)))
    adj, ws, wn, bias, cot = held
    early = call(
        early_kernel,
        [VMEM] * 4,
        (sds((f_in, TILE), F32), sds((8, TILE), F32), sds((TILE, f_out), F32)),
    )(own, adj, ws, bias)
    near, far, early = lax.optimization_barrier((near, far, early))
    act, grad, keep, send, back, scaled = call(
        forward_kernel,
        [SMEM] + [VMEM] * 10,
        (sds((TILE, f_out)), sds((TILE, f_out)), wide, sds((2 * f_in + f_out, TILE)), wide, wide),
    )(core, near, far, own, adj, ws, wn, cot, *early)
    recv = swap(send)
    s_far = across(scaled)
    partial, act = call(
        partial_kernel, [VMEM] * 4, (sds((N_X, f_in + TAIL, TILE)), sds((TILE, f_out)))
    )(keep, grad, recv, act)
    from_x = exchange(partial, "x")
    feats = call(feat_kernel, [SMEM] + [VMEM] * 5, sds((N_LINE, 2 * width, TILE)))(
        core, recv, s_far, scaled, adj, back
    )
    from_y = exchange(call(x_kernel, [VMEM], sds((N_Y, ROWS + TAIL, TILE)))(from_x), "y")
    from_line = exchange(call(y_kernel, [VMEM], sds((N_LINE, THIRD + TAIL, TILE)))(from_y), LINE)
    from_line, feats = lax.optimization_barrier((from_line, feats))
    to_y_again, bias_sum = call(
        lambda *refs: line_kernel(scale, *refs),
        [VMEM],
        (sds((N_Y, THIRD, TILE)), sds((1, f_out), F32)),
    )(from_line)
    column = exchange(to_y_again, "y").reshape(N_Y * THIRD, TILE)
    to_block = call(join_kernel, [VMEM] * 2, sds((N_LINE, N_Y * THIRD + 2 * width, TILE)))(column, feats)
    block = exchange(to_block, BLOCK)
    other = swap(block)
    whole = sds((width, n_rows), F32)
    room = [
        pltpu.VMEM((f_in, f_out), F32),
        dma((N_X,)),
        pltpu.VMEM((N_LINE, width, TILE), F32),
        dma((N_LINE,)),
    ]
    partly = call(
        own_kernel, [SMEM, VMEM], (weight, weight, whole), room, out_specs=(ANY,) * 3
    )(core, block)
    grad_self, grad_neigh, gf = call(
        other_kernel,
        [SMEM, VMEM] + [ANY] * 3,
        (weight, weight, whole),
        room,
        out_specs=(ANY,) * 3,
        input_output_aliases={2: 0, 3: 1, 4: 2},
    )(core, other, *partly)
    return act, grad_self, grad_neigh, bias_sum.reshape(f_out), gf.T


def solution(mesh):
    grid = Mesh(mesh.devices.reshape(SIZES), AXES)
    in_specs = (P(GRAPH, FEAT), P(GRAPH, None), P(), P(), P(), P(GRAPH + FEAT, None))
    out_specs = (P(GRAPH + FEAT, None), P(), P(), P(), P(GRAPH, FEAT))
    return jax.shard_map(local, mesh=grid, in_specs=in_specs, out_specs=out_specs, check_vma=False)
```
